256 devices in a mesh: fx: 32 (over z, x), fy: 8 (over y, core).
Axes of the slice: x: 4, y: 4, z: 8, core: 2. Of those that a mesh axis runs over, the one named last changes fastest.
Arguments:
- sky_image: float32 [32, 65536], P('fy', 'fx'), may hold values from -6 to 6
- col_off: int32 [32], replicated, may hold values from 0 to 65535
- row_off: int32 [8], replicated, may hold values from 0 to 65535
- layer_counts: int32 [32, 8], P('fx', 'fy'), may hold values from 1 to 8
- w_steps: int32 [32, 8, 8], P('fx', 'fy'), may hold values from 1 to 4
- live_blocks: int32 [32, 8], P('fx', 'fy'), may hold values from 1 to 16
- block_codes: int32 [32, 8, 16], P('fx', 'fy'), may hold values from 0 to 839
- vis_coords: float32 [32, 8, 16, 2, 128], P('fx', 'fy'), may hold values from 0 to 1
Outputs:
- visibilities: float32 [32, 8, 16, 2, 128], P('fx', 'fy')
The draws below stay inside these ranges and needn't reach their ends.
All inputs are finite; a program needn't handle non-finite values.
Results may differ from the reference program's by a relative error of at most 0.018.
Values may be sent and summed in bfloat16 or wider, within the bound.
A program may use at most 64 MiB of HBM per device.

```python
import math
import jax
import jax.numpy as jnp
from jax import lax

FC = 2048
SG = 1024
NSKY = 65536
FR = 4
WL = 8
NB = 16
NV = 128
SG0 = 32
NSKY0 = 32
NSKY1 = 65536
N_FX = 32
N_FY = 8


def touch_ends(drawn, own_key, least, top_value):
    longest = drawn.shape.index(max(drawn.shape))
    spots = []
    for shift in (0, 1):
        where = [jax.random.randint(jax.random.fold_in(own_key, axis), (), 0, length) for axis, length in enumerate(drawn.shape)]
        where[longest] = (where[longest] + shift) % drawn.shape[longest]
        spots.append(tuple(where))
    return drawn.at[spots[0]].set(least).at[spots[1]].set(top_value)


def block_scale(own_key, extent, split, least, largest):
    def one(position, blocks):
        draws = jax.random.uniform(jax.random.fold_in(jax.random.fold_in(own_key, 6), position), (blocks,), jnp.float32, least / len(split), largest / len(split))
        return jnp.repeat(jnp.exp(draws), extent[position] // blocks).reshape((-1,) + (1,) * (len(extent) - position - 1))

    gain = one(*split[0])
    for cut in split[1:]:
        gain = gain * one(*cut)
    return gain


def normal_values(key, extent, scale, reach, cuts=(), kind=jnp.bfloat16):
    result = scale * jax.random.normal(key, extent, jnp.float32)
    if cuts:
        result = result * block_scale(key, extent, cuts, -0.22, 0.18)
    return jnp.clip(result, -reach, reach).astype(kind)


def setup_inputs(seed: int = 0) -> dict:
    arg_keys = jax.random.split(jax.random.key(seed), 9)
    sky_image = normal_values(arg_keys[0], (NSKY0, NSKY1), 1.0, 6.0, ((0, 8), (1, 32)), jnp.float32)
    col_off = touch_ends(jax.random.randint(arg_keys[1], (N_FX,), 0, NSKY1), jax.random.fold_in(arg_keys[1], 1), 0, NSKY1 - 1).astype(jnp.int32)
    row_off = touch_ends(jax.random.randint(arg_keys[2], (N_FY,), 0, NSKY), jax.random.fold_in(arg_keys[2], 1), 0, NSKY - 1).astype(jnp.int32)
    layer_counts = touch_ends(jax.random.randint(arg_keys[3], (N_FX, N_FY), 1, WL + 1), jax.random.fold_in(arg_keys[3], 1), 1, WL).astype(jnp.int32)
    w_steps = touch_ends(jax.random.randint(arg_keys[4], (N_FX, N_FY, WL), 1, 5), jax.random.fold_in(arg_keys[4], 1), 1, 4).astype(jnp.int32)
    live_blocks = touch_ends(jax.random.randint(arg_keys[5], (N_FX, N_FY), 1, NB + 1), jax.random.fold_in(arg_keys[5], 1), 1, NB).astype(jnp.int32)
    block_codes = touch_ends(jax.random.randint(arg_keys[6], (N_FX, N_FY, NB), 0, 840), jax.random.fold_in(arg_keys[6], 1), 0, 839).astype(jnp.int32)
    vis_coords = jnp.clip(1.0 * jax.random.uniform(arg_keys[7], (N_FX, N_FY, NB, 2, NV), jnp.float32) ** block_scale(arg_keys[7], (N_FX, N_FY, NB, 2, NV), ((0, 32), (1, 8)), -0.2, 0.2), 0.0, 1.0)
    return {"sky_image": sky_image, "col_off": col_off, "row_off": row_off, "layer_counts": layer_counts, "w_steps": w_steps, "live_blocks": live_blocks, "block_codes": block_codes, "vis_coords": vis_coords}


two_pi = 6.283185307179586
coarse_step = 32

def mulmod(factor_a, factor_b, modulus):
    high_part = factor_b // 256
    low_part = factor_b % 256
    reduced = factor_a * high_part % modulus
    return (reduced * 256 + factor_a * low_part) % modulus

def build_layers(subgrid, steps_list):
    rows_grid = subgrid.shape[0]
    cols_grid = subgrid.shape[1] // 2
    depths = jnp.cumsum(steps_list).astype(jnp.int32)
    centre_rows = jnp.arange(rows_grid, dtype=jnp.int32) - rows_grid // 2
    centre_cols = jnp.arange(cols_grid, dtype=jnp.int32) - cols_grid // 2
    radial = centre_rows[:, None] * centre_rows[:, None] + centre_cols[None, :] * centre_cols[None, :]
    screen = math.pi / cols_grid * (depths[:, None, None] * radial[None, :, :] % (2 * cols_grid)).astype(jnp.float32)
    cosine = jnp.cos(screen)
    sine_part = jnp.sin(screen)
    grid_real = subgrid[:, :cols_grid]
    grid_imag = subgrid[:, cols_grid:]
    layer_real = grid_real[None] * cosine - grid_imag[None] * sine_part
    layer_imag = grid_real[None] * sine_part + grid_imag[None] * cosine
    return jnp.concatenate([layer_real, layer_imag], axis=1).astype(jnp.bfloat16)

def kernel_visibilities(stacked, u_pos, v_pos):
    rows_grid = stacked.shape[0] // 2
    cols_grid = stacked.shape[1]
    count_vis = v_pos.shape[0]
    coarse = (jnp.arange(cols_grid // coarse_step, dtype=jnp.int32) * coarse_step).astype(jnp.float32)
    fine_part = jnp.arange(coarse_step, dtype=jnp.int32).astype(jnp.float32)
    coarse_angle = two_pi * coarse[:, None] * v_pos[None, :]
    fine_angle = two_pi * fine_part[:, None] * v_pos[None, :]
    coarse_cos = jnp.cos(coarse_angle)[:, None, :]
    coarse_sin = jnp.sin(coarse_angle)[:, None, :]
    fine_cos = jnp.cos(fine_angle)[None, :, :]
    fine_sin = jnp.sin(fine_angle)[None, :, :]
    kernel_real = (coarse_cos * fine_cos - coarse_sin * fine_sin).reshape(cols_grid, count_vis)
    kernel_imag = (coarse_sin * fine_cos + coarse_cos * fine_sin).reshape(cols_grid, count_vis)
    kernel = jnp.concatenate([kernel_real, kernel_imag], axis=1).astype(jnp.bfloat16)
    products = jnp.dot(stacked, kernel, preferred_element_type=jnp.float32)
    part_real = products[:rows_grid, :count_vis] - products[rows_grid:, count_vis:]
    part_imag = products[:rows_grid, count_vis:] + products[rows_grid:, :count_vis]
    row_angle = two_pi * jnp.arange(rows_grid, dtype=jnp.int32).astype(jnp.float32)[:, None] * u_pos[None, :]
    row_cos = jnp.cos(row_angle)
    row_sin = jnp.sin(row_angle)
    vis_scale = 1.0 / math.sqrt(rows_grid * cols_grid)
    vis_real = lax.optimization_barrier(jnp.sum(row_cos * part_real - row_sin * part_imag, axis=0)) * vis_scale
    vis_imag = lax.optimization_barrier(jnp.sum(row_cos * part_imag + row_sin * part_real, axis=0)) * vis_scale
    return jnp.stack([vis_real, vis_imag])

def reference(sky_image, col_off, row_off, layer_counts, w_steps, live_blocks, block_codes, vis_coords):
    total_cols = FC * N_FX
    total_rows = FR * N_FY
    band_cols = jnp.arange(SG, dtype=jnp.int32)
    wave_cols = ((col_off[:, None] + band_cols[None, :]) % total_cols).astype(jnp.int32)
    col_phase = -two_pi / total_cols
    col_scale = 1.0 / math.sqrt(total_cols)

    def add_facet(carry, facet_index):
        pieces = lax.dynamic_slice_in_dim(sky_image, facet_index * FC, FC, 1)
        spectrum = jnp.fft.fft(pieces, n=total_cols, axis=1)
        chosen = jnp.take(spectrum, wave_cols.reshape(-1), axis=1).reshape(total_rows, N_FX, SG)
        turned = mulmod(facet_index * FC % total_cols, wave_cols, total_cols)
        angles = col_phase * turned.astype(jnp.float32)
        post_cos = jnp.cos(angles)[None]
        post_sin = jnp.sin(angles)[None]
        real_part = jnp.real(chosen)
        imag_part = jnp.imag(chosen)
        band_real = (real_part * post_cos - imag_part * post_sin) * col_scale
        band_imag = (real_part * post_sin + imag_part * post_cos) * col_scale
        rounded = lax.optimization_barrier(jnp.stack([band_real, band_imag]).astype(jnp.bfloat16))
        return (carry + rounded.astype(jnp.float32), None)
    band_zero = jnp.zeros((2, total_rows, N_FX, SG), jnp.float32)
    band_total, unused = lax.scan(add_facet, band_zero, jnp.arange(N_FX, dtype=jnp.int32))
    strip_data = band_total.astype(jnp.bfloat16).astype(jnp.float32)
    row_phase = -two_pi / NSKY
    row_scale = 1.0 / math.sqrt(total_rows)
    wave_rows = ((row_off[:, None] + jnp.arange(SG0, dtype=jnp.int32)[None, :]) % NSKY).astype(jnp.int32)
    cell_rows = jnp.arange(total_rows, dtype=jnp.int32)
    sky_rows = (cell_rows // FR * (NSKY // N_FY) + cell_rows % FR).astype(jnp.int32)
    row_angles = row_phase * mulmod(sky_rows[None, None, :], wave_rows[:, :, None], NSKY).astype(jnp.float32)
    tab_cos = jnp.cos(row_angles)
    tab_sin = jnp.sin(row_angles)

    def contract(table_part, data_part):
        return jnp.einsum('rmx,xsj->srmj', table_part, data_part, precision=lax.Precision.HIGHEST)

    def add_row(carry, facet_row):
        data_real = lax.dynamic_slice_in_dim(strip_data[0], facet_row * FR, FR, 0)
        data_imag = lax.dynamic_slice_in_dim(strip_data[1], facet_row * FR, FR, 0)
        part_cos = lax.dynamic_slice_in_dim(tab_cos, facet_row * FR, FR, 2)
        part_sin = lax.dynamic_slice_in_dim(tab_sin, facet_row * FR, FR, 2)
        term_real = (contract(part_cos, data_real) - contract(part_sin, data_imag)) * row_scale
        term_imag = (contract(part_cos, data_imag) + contract(part_sin, data_real)) * row_scale
        rounded = lax.optimization_barrier(jnp.stack([term_real, term_imag], axis=2).astype(jnp.bfloat16))
        return (carry + rounded.astype(jnp.float32), None)
    grid_zero = jnp.zeros((N_FX, N_FY, 2, SG0, SG), jnp.float32)
    grids, unused_rows = lax.scan(add_row, grid_zero, jnp.arange(N_FY, dtype=jnp.int32))
    flat_grids = grids.reshape(N_FX * N_FY, 2, SG0, SG)

    def per_subgrid(packed):
        grid_pair, steps_list, count_here, live_here, codes_here, coords_here = packed
        subgrid = jnp.concatenate([grid_pair[0], grid_pair[1]], axis=1)
        layers = build_layers(subgrid, steps_list)

        def per_block(inputs):
            block_index, code_value, coords = inputs
            stacked = lax.dynamic_index_in_dim(layers, code_value % count_here, 0, keepdims=False)
            values = kernel_visibilities(stacked, coords[0], coords[1])
            return jnp.where(block_index < live_here, values, jnp.zeros_like(values))
        return lax.map(per_block, (jnp.arange(NB, dtype=jnp.int32), codes_here, coords_here))
    outputs = lax.map(per_subgrid, (flat_grids, w_steps.reshape(N_FX * N_FY, WL), layer_counts.reshape(-1), live_blocks.reshape(-1), block_codes.reshape(N_FX * N_FY, NB), vis_coords.reshape(N_FX * N_FY, NB, 2, NV)))
    return outputs.reshape(N_FX, N_FY, NB, 2, NV)
```

```python
import math

import jax
import jax.numpy as jnp
from jax import lax
from jax.sharding import PartitionSpec as P

SG = 1024
NSKY = 65536


two_pi = 6.283185307179586
coarse_step = 32


def mulmod(factor_a, factor_b, modulus):
    high_part = factor_b // 256
    low_part = factor_b % 256
    reduced = factor_a * high_part % modulus
    return (reduced * 256 + factor_a * low_part) % modulus


def precise(matrix_a, matrix_b):
    return jnp.dot(
        matrix_a, matrix_b, precision=lax.Precision.HIGHEST, preferred_element_type=jnp.float32
    )


def pick_offset(offsets, selector):
    slots = jnp.arange(offsets.shape[0], dtype=jnp.int32)
    chosen = jnp.sum(jnp.where(selector[:, None] == slots[None, :], offsets[None, :], 0), axis=1)
    return chosen


def build_layers(subgrid, steps_list):
    rows_grid = subgrid.shape[0]
    cols_grid = subgrid.shape[1] // 2
    slots = jnp.arange(steps_list.shape[0], dtype=jnp.int32)
    depths = jnp.sum(jnp.where(slots[None, :] <= slots[:, None], steps_list[None, :], 0), axis=1)
    centre_rows = jnp.arange(rows_grid, dtype=jnp.int32) - rows_grid // 2
    centre_cols = jnp.arange(cols_grid, dtype=jnp.int32) - cols_grid // 2
    radial = (
        centre_rows[:, None] * centre_rows[:, None] + centre_cols[None, :] * centre_cols[None, :]
    )
    screen = (
        math.pi
        / cols_grid
        * (depths[:, None, None] * radial[None, :, :] % (2 * cols_grid)).astype(jnp.float32)
    )
    cosine = jnp.cos(screen)
    sine_part = jnp.sin(screen)
    grid_real = subgrid[:, :cols_grid]
    grid_imag = subgrid[:, cols_grid:]
    layer_real = grid_real[None] * cosine - grid_imag[None] * sine_part
    layer_imag = grid_real[None] * sine_part + grid_imag[None] * cosine
    return jnp.concatenate([layer_real, layer_imag], axis=1).astype(jnp.bfloat16)


def kernel_visibilities(stacked, u_pos, v_pos):
    rows_grid = stacked.shape[0] // 2
    cols_grid = stacked.shape[1]
    count_vis = v_pos.shape[0]
    coarse = (jnp.arange(cols_grid // coarse_step, dtype=jnp.int32) * coarse_step).astype(
        jnp.float32
    )
    fine_part = jnp.arange(coarse_step, dtype=jnp.int32).astype(jnp.float32)
    coarse_angle = two_pi * coarse[:, None] * v_pos[None, :]
    fine_angle = two_pi * fine_part[:, None] * v_pos[None, :]
    coarse_cos = jnp.cos(coarse_angle)[:, None, :]
    coarse_sin = jnp.sin(coarse_angle)[:, None, :]
    fine_cos = jnp.cos(fine_angle)[None, :, :]
    fine_sin = jnp.sin(fine_angle)[None, :, :]
    kernel_real = (coarse_cos * fine_cos - coarse_sin * fine_sin).reshape(cols_grid, count_vis)
    kernel_imag = (coarse_sin * fine_cos + coarse_cos * fine_sin).reshape(cols_grid, count_vis)
    kernel = jnp.concatenate([kernel_real, kernel_imag], axis=1).astype(jnp.bfloat16)
    products = jnp.dot(stacked, kernel, preferred_element_type=jnp.float32)
    part_real = products[:rows_grid, :count_vis] - products[rows_grid:, count_vis:]
    part_imag = products[:rows_grid, count_vis:] + products[rows_grid:, :count_vis]
    row_angle = (
        two_pi
        * jnp.arange(rows_grid, dtype=jnp.int32).astype(jnp.float32)[:, None]
        * u_pos[None, :]
    )
    row_cos = jnp.cos(row_angle)
    row_sin = jnp.sin(row_angle)
    vis_scale = 1.0 / math.sqrt(rows_grid * cols_grid)
    vis_real = jnp.sum(row_cos * part_real - row_sin * part_imag, axis=0) * vis_scale
    vis_imag = jnp.sum(row_cos * part_imag + row_sin * part_real, axis=0) * vis_scale
    return jnp.stack([vis_real, vis_imag])


def per_device(
    sky_image, col_off, row_off, layer_counts, w_steps, live_blocks, block_codes, vis_coords
):
    rows_here, facet_cols = sky_image.shape
    num_cols = lax.axis_size("fx")
    num_rows = lax.axis_size("fy")
    col_index = lax.axis_index("fx")
    row_index = lax.axis_index("fy")
    total_cols = facet_cols * num_cols
    total_rows = rows_here * num_rows
    block_width = min(facet_cols, 128)
    col_phase = -two_pi / total_cols
    col_scale = 1.0 / math.sqrt(total_cols)
    band_cols = jnp.arange(SG, dtype=jnp.int32)

    def one_turn(carry, turn_index):
        acc_real, acc_imag = carry
        local_cols = turn_index * block_width + jnp.arange(block_width, dtype=jnp.int32)
        pieces = lax.dynamic_slice_in_dim(sky_image, turn_index * block_width, block_width, 1)
        pre_angle = col_phase * (local_cols[None, :] * col_off[:, None] % total_cols).astype(
            jnp.float32
        )
        pre_real = (jnp.cos(pre_angle)[:, None, :] * pieces[None, :, :]).reshape(
            num_cols * rows_here, block_width
        )
        pre_imag = (jnp.sin(pre_angle)[:, None, :] * pieces[None, :, :]).reshape(
            num_cols * rows_here, block_width
        )
        table_angle = col_phase * (local_cols[:, None] * band_cols[None, :] % total_cols).astype(
            jnp.float32
        )
        table_real = jnp.cos(table_angle)
        table_imag = jnp.sin(table_angle)
        acc_real = acc_real + precise(pre_real, table_real) - precise(pre_imag, table_imag)
        acc_imag = acc_imag + precise(pre_real, table_imag) + precise(pre_imag, table_real)
        return ((acc_real, acc_imag), None)

    zeros_acc = jnp.zeros((num_cols * rows_here, SG), jnp.float32)
    turn_list = jnp.arange(facet_cols // block_width, dtype=jnp.int32)
    (sum_real, sum_imag), unused = lax.scan(one_turn, (zeros_acc, zeros_acc), turn_list)
    wave_cols = (col_off[:, None] + band_cols[None, :]) % total_cols
    turned = mulmod(col_index * facet_cols % total_cols, wave_cols, total_cols)
    post_angle = col_phase * turned.astype(jnp.float32)
    post_cos = jnp.cos(post_angle)[:, None, :]
    post_sin = jnp.sin(post_angle)[:, None, :]
    sum_real = sum_real.reshape(num_cols, rows_here, SG)
    sum_imag = sum_imag.reshape(num_cols, rows_here, SG)
    band_real = (sum_real * post_cos - sum_imag * post_sin) * col_scale
    band_imag = (sum_real * post_sin + sum_imag * post_cos) * col_scale
    band_data = jnp.stack([band_real, band_imag], axis=2)
    received = lax.all_to_all(
        band_data.astype(jnp.bfloat16), "fx", split_axis=0, concat_axis=0, tiled=True
    )
    strips = jnp.sum(received.astype(jnp.float32), axis=0)
    strips = strips.astype(jnp.bfloat16)
    row_phase = -two_pi / NSKY
    row_scale = 1.0 / math.sqrt(total_rows)
    facet_stride = NSKY // num_rows
    strip_real = strips[:, 0, :].astype(jnp.float32)
    strip_imag = strips[:, 1, :].astype(jnp.float32)
    own_cells = row_index * facet_stride + jnp.arange(rows_here, dtype=jnp.int32)
    index_rows = jnp.arange(lax.axis_size("fy") * total_rows, dtype=jnp.int32)
    wave_rows = (pick_offset(row_off, index_rows // total_rows) + index_rows % total_rows) % NSKY
    angles = row_phase * mulmod(own_cells[None, :], wave_rows[:, None], NSKY).astype(jnp.float32)
    tab_cos = jnp.cos(angles)
    tab_sin = jnp.sin(angles)
    term_real = (precise(tab_cos, strip_real) - precise(tab_sin, strip_imag)) * row_scale
    term_imag = (precise(tab_cos, strip_imag) + precise(tab_sin, strip_real)) * row_scale
    subgrid = lax.psum_scatter(
        jnp.concatenate([term_real, term_imag], axis=1).astype(jnp.bfloat16),
        "fy",
        scatter_dimension=0,
        tiled=True,
    ).astype(jnp.float32)
    layers = build_layers(subgrid, w_steps[0, 0, :])
    count_here = layer_counts[0, 0]
    codes_here = block_codes[0, 0]
    coords_here = vis_coords[0, 0]

    def degrid(block_index, buffer):
        plane_index = (
            lax.dynamic_index_in_dim(codes_here, block_index, 0, keepdims=False) % count_here
        )
        stacked = lax.dynamic_index_in_dim(layers, plane_index, 0, keepdims=False)
        coords = lax.dynamic_index_in_dim(coords_here, block_index, 0, keepdims=False)
        values = kernel_visibilities(stacked, coords[0], coords[1])
        return lax.dynamic_update_index_in_dim(buffer, values, block_index, 0)

    initial = jnp.zeros(coords_here.shape, jnp.float32)
    result = lax.fori_loop(0, live_blocks[0, 0], degrid, initial)
    return result[None, None]


def solution(mesh):
    placed = (
        P("fy", "fx"),
        P(),
        P(),
        P("fx", "fy"),
        P("fx", "fy", None),
        P("fx", "fy"),
        P("fx", "fy", None),
        P("fx", "fy", None, None, None),
    )
    return jax.shard_map(
        per_device,
        mesh=mesh,
        in_specs=placed,
        out_specs=P("fx", "fy", None, None, None),
        check_vma=False,
    )
```

```python
import functools

import jax
import jax.numpy as jnp
import numpy as np
from jax import lax
from jax.experimental import pallas as pl
from jax.experimental.pallas import tpu as pltpu
from jax.sharding import PartitionSpec as P

MESH = pl.DeviceIdType.MESH
SG = 1024
NSKY = 65536
NB = 16
NV = 128
SG0 = 32
NX = 4
NZ = 8
NQ = 8
HALF = SG // 2
F32 = jnp.float32
BF16 = jnp.bfloat16
SIN = (3.141592502593994, -5.167698860168457, 2.5499982833862305, -0.59855055809021, 0.0807478204369545, -0.00608947454020381)
COS = (1.0, -4.93480110168457, 4.058694839477539, -1.3351584672927856, 0.23502980172634125, -0.025358984246850014, 0.0015939107397571206)


def cis(turns):
    near = turns - jnp.floor(turns + 0.5)
    y = near + near
    z = y * y
    sine = jnp.full_like(z, SIN[-1])
    for c in SIN[-2::-1]:
        sine = sine * z + c
    cosine = jnp.full_like(z, COS[-1])
    for c in COS[-2::-1]:
        cosine = cosine * z + c
    return cosine, sine * y


def dft_table():
    row = np.arange(NZ * 32)
    b = 128 * (row // 32) + 2 * (row % 16) + (row // 16) % 2
    angle = (b[:, None] * np.arange(SG)[None, :]) % SG * (2 * np.pi / SG)
    return np.concatenate([np.cos(angle), -np.sin(angle)], axis=1).astype(BF16)


def iota(shape, axis):
    return lax.broadcasted_iota(jnp.int32, shape, axis)


def kernel(
    sky_h, col_h, row_h, cnt_h, ws_h, live_h, codes_h, crd_h, tab_h, out,
    sky, tmp, tab, crd, col, rows, cnt, ws, live, codes, gath, spec, w8, tw, ybuf, part, got, strips, ker, vtab,
    load_sem, send1, recv1, send2, recv2, send3, recv3,
):
    fx, fy = lax.axis_index("fx"), lax.axis_index("fy")
    z, x = fx // NX, lax.rem(fx, NX)

    pairs = [(sky_h, sky), (col_h, col), (row_h, rows), (cnt_h, cnt), (ws_h, ws), (live_h, live), (codes_h, codes), (crd_h, crd), (tab_h, tab)]
    loads = [pltpu.make_async_copy(a, b, load_sem.at[i]) for i, (a, b) in enumerate(pairs)]
    for load in loads:
        load.start()

    along_z = [(lax.rem(z + d, NZ) * NX + x, fy) for d in range(1, NZ)]
    along_x = [(z * NX + lax.rem(x + d, NX), fy) for d in range(1, NX)]
    along_q = [(fx, lax.rem(fy + d, NQ)) for d in range(1, NQ)]
    barrier = pltpu.get_barrier_semaphore()
    for peer in along_z + along_x + along_q:
        pl.semaphore_signal(barrier, inc=1, device_id=peer, device_id_type=MESH)

    loads[0].wait()
    for j in range(16):
        tmp[4 * j : 4 * j + 4, :] = sky[:, 128 * j : 128 * j + 128]
    left = iota((16, 128), 1) < 64
    line = [tmp[pl.ds(i, 16, stride=4), :] for i in range(4)]
    turned = [pltpu.roll(a, 64, 1) for a in line]
    halves = []
    for i in (0, 2):
        low = jnp.where(left, line[i], turned[i + 1])
        high = jnp.where(left, turned[i], line[i + 1])
        halves.append(jnp.concatenate([low, high], axis=0))
    gath[z] = jnp.concatenate(halves, axis=1).astype(BF16)

    pl.semaphore_wait(barrier, len(along_z) + len(along_x) + len(along_q))

    def phase1(d, slot):
        return pltpu.make_async_remote_copy(
            src_ref=gath.at[slot], dst_ref=gath.at[slot], send_sem=send1.at[d], recv_sem=recv1.at[d],
            device_id=along_z[d - 1], device_id_type=MESH,
        )

    sent1 = [phase1(d, z) for d in (4, 3, 5, 2, 6, 1, 7)]
    for copy in sent1:
        copy.start()
    for load in loads[1:]:
        load.wait()

    kappa = iota((8, SG), 1)
    c0 = iota((8, SG), 0)

    def wave(off):
        return off + jnp.bitwise_and(kappa - off, SG - 1)

    for d in range(NX):
        k = wave(col[z * NX + lax.rem(x + d, NX)])
        cosine, sine = cis(jnp.bitwise_and(k * 8, NSKY - 1).astype(F32) * (1.0 / NSKY))
        w8[d, 0] = cosine
        w8[d, 1] = -sine
        cosine, sine = cis(jnp.bitwise_and(c0 * k + 2048 * x * kappa, NSKY - 1).astype(F32) * (1.0 / NSKY))
        tw[d, 0] = cosine
        tw[d, 1] = -sine

    r = iota((128, 64), 0)
    m = iota((128, 64), 1)
    q, ri, i = jnp.bitwise_and(r, 63) // 8, jnp.bitwise_and(r, 7) // 4, jnp.bitwise_and(r, 3)
    turn = jnp.bitwise_and((q * (NSKY // NQ) + i) * (rows[fy] + jnp.bitwise_and(m, 31)), NSKY - 1)
    quarter = ri - (r >= 64).astype(jnp.int32) + (m >= 32).astype(jnp.int32)
    wide = cis(quarter.astype(F32) * 0.25 - turn.astype(F32) * (1.0 / NSKY))[0].astype(BF16)

    count = cnt[0, 0]
    g = iota((32, NV), 0)
    centre = g - 512
    middle = g - 16

    def tables(b):
        plane = lax.rem(codes[0, 0, b], count)
        depth = jnp.int32(0)
        for layer in range(8):
            depth = depth + jnp.where(layer <= plane, ws[0, 0, layer], 0)
        u = crd[0, 0, b, 0:1, :]
        v = crd[0, 0, b, 1:2, :]
        screen = jnp.bitwise_and(depth * middle * middle, 2047).astype(F32) * (1.0 / 2048)
        wave_real, wave_imag = cis(g.astype(F32) * u + screen)
        both = jnp.concatenate([wave_real, wave_imag], axis=0).astype(BF16)
        vtab[b] = jnp.dot(wide, both, preferred_element_type=F32)
        screen = jnp.bitwise_and(depth * centre * centre, 2047).astype(F32) * (1.0 / 2048)
        real, imag = cis(g.astype(F32) * v + screen)
        step = jnp.bitwise_and(depth * (g + 16), 31).astype(F32) * (1.0 / 32)
        step_real, step_imag = cis(32.0 * v + step)
        return real, imag, step_real, step_imag

    def fill(b2, carry):
        blocks = [2 * b2, 2 * b2 + 1]
        state = [tables(b) for b in blocks]
        fixed = [s[2:] for s in state]

        def stride(h, values):
            result = []
            for b, (real, imag), (sr, si) in zip(blocks, values, fixed):
                at = pl.ds(pl.multiple_of(32 * h, 32), 32)
                ker[b, at, 0:NV] = real.astype(BF16)
                ker[b, at, NV : 2 * NV] = imag.astype(BF16)
                result.append((real * sr - imag * si, real * si + imag * sr))
            return tuple(result)

        lax.fori_loop(0, 32, stride, tuple(s[:2] for s in state), unroll=4)
        return carry

    lax.fori_loop(0, NB // 2, fill, 0)

    for d in range(1, NZ):
        phase1(d, lax.rem(z + NZ - d, NZ)).wait_recv()

    sky_t = gath[...].reshape(NZ * 32, 256)
    spec[...] = lax.dot_general(sky_t, tab[...], (((0,), (0,)), ((), ())), preferred_element_type=F32)
    pick_row = iota((8, 64), 0)
    pick_col = iota((8, 64), 1)
    pick = jnp.where(
        (pick_col // 16 == jnp.bitwise_and(pick_row, 3)) & (jnp.bitwise_and(pick_col // 8, 1) == pick_row // 4), 1.0, 0.0
    ).astype(BF16)

    def phase2(d):
        return pltpu.make_async_remote_copy(
            src_ref=part.at[d], dst_ref=got.at[d], send_sem=send2.at[d], recv_sem=recv2.at[d],
            device_id=along_x[d - 1], device_id_type=MESH,
        )

    own = None
    for d in (2, 1, 3, 0):
        def facet_row(x0, carry):
            for lo in (0, HALF):
                cols = slice(lo, lo + HALF)
                wr, wi = w8[d, 0, :, cols], w8[d, 1, :, cols]

                def at(c1, plus):
                    return spec[pl.ds(pl.multiple_of(x0 * 64 + 8 * c1, 8), 8), lo + plus : lo + plus + HALF]

                ar, ai = at(7, 0), at(7, SG)
                for c1 in range(6, -1, -1):
                    ar, ai = ar * wr - ai * wi + at(c1, 0), ar * wi + ai * wr + at(c1, SG)
                tr, ti = tw[d, 0, :, cols], tw[d, 1, :, cols]
                both = jnp.concatenate([ar * tr - ai * ti, ar * ti + ai * tr], axis=0)
                ybuf[d, pl.ds(pl.multiple_of(x0 * 16, 16), 16), cols] = both.astype(BF16)
            return carry

        lax.fori_loop(0, 4, facet_row, 0)
        strip = jnp.dot(pick, ybuf[d], preferred_element_type=F32)
        packed = jnp.concatenate([strip[:, :HALF], strip[:, HALF:]], axis=0)
        if d:
            part[d] = packed.astype(BF16)
            phase2(d).start()
        else:
            own = packed
    for d in (1, 3, 2):
        phase2(d).wait_recv()
        own = own + got[d].astype(F32)

    flat = jnp.concatenate([own[:8], own[8:]], axis=1)
    flat = pltpu.roll(flat, jnp.bitwise_and(SG - jnp.bitwise_and(col[fx], SG - 1), SG - 1), 1)
    strips[fy] = jnp.concatenate([flat[:, :HALF], flat[:, HALF:]], axis=0).astype(BF16)

    def phase3(d, slot):
        return pltpu.make_async_remote_copy(
            src_ref=strips.at[slot], dst_ref=strips.at[slot], send_sem=send3.at[d], recv_sem=recv3.at[d],
            device_id=along_q[d - 1], device_id_type=MESH,
        )

    sent3 = [phase3(d, fy) for d in (4, 3, 5, 2, 6, 1, 7)]
    for copy in sent3:
        copy.start()
    for d in range(1, NQ):
        phase3(d, lax.rem(fy + NQ - d, NQ)).wait_recv()
    wide_strips = strips[...].astype(F32)
    left_half = wide_strips[:, 0:8, :].reshape(64, HALF)
    right_half = wide_strips[:, 8:16, :].reshape(64, HALF)
    lines = jnp.concatenate([left_half, right_half], axis=1).astype(BF16)

    def degrid(b, carry):
        prod = jnp.dot(lines, ker[b], preferred_element_type=F32)
        vr, vi = vtab[b, 0:64, :], vtab[b, 64:128, :]
        pr, pi = prod[:, :NV], prod[:, NV:]
        scale = jnp.where(b < live[0, 0], 2.0**-18, 0.0)
        out[0, 0, b, 0:1, :] = jnp.sum(vr * pr - vi * pi, axis=0, keepdims=True) * scale
        out[0, 0, b, 1:2, :] = jnp.sum(vr * pi + vi * pr, axis=0, keepdims=True) * scale
        return carry

    lax.fori_loop(0, NB, degrid, 0, unroll=4)

    for copy in sent1:
        copy.wait_send()
    for d in (2, 1, 3):
        phase2(d).wait_send()
    for copy in sent3:
        copy.wait_send()


def per_device(sky, col, rows, cnt, ws, live, codes, crd):
    hbm = pl.BlockSpec(memory_space=pl.ANY)
    dma = pltpu.SemaphoreType.DMA
    return pl.pallas_call(
        kernel,
        out_shape=jax.ShapeDtypeStruct((1, 1, NB, 2, NV), F32),
        in_specs=[hbm] * 9,
        out_specs=pl.BlockSpec(memory_space=pltpu.VMEM),
        scratch_shapes=[
            pltpu.VMEM((4, 2048), F32),
            pltpu.VMEM((64, 128), F32),
            pltpu.VMEM((256, 2 * SG), BF16),
            pltpu.VMEM((1, 1, NB, 2, NV), F32),
            pltpu.SMEM((32,), jnp.int32),
            pltpu.SMEM((8,), jnp.int32),
            pltpu.SMEM((1, 1), jnp.int32),
            pltpu.SMEM((1, 1, 8), jnp.int32),
            pltpu.SMEM((1, 1), jnp.int32),
            pltpu.SMEM((1, 1, NB), jnp.int32),
            pltpu.VMEM((NZ, 32, 256), BF16),
            pltpu.VMEM((256, 2 * SG), F32),
            pltpu.VMEM((NX, 2, 8, SG), F32),
            pltpu.VMEM((NX, 2, 8, SG), F32),
            pltpu.VMEM((NX, 64, SG), BF16),
            pltpu.VMEM((NX, 16, HALF), BF16),
            pltpu.VMEM((NX, 16, HALF), BF16),
            pltpu.VMEM((NQ, 16, HALF), BF16),
            pltpu.VMEM((NB, SG, 2 * NV), BF16),
            pltpu.VMEM((NB, 128, NV), F32),
            dma((9,)), dma((NZ,)), dma((NZ,)), dma((NX,)), dma((NX,)), dma((NQ,)), dma((NQ,)),
        ],
        compiler_params=pltpu.CompilerParams(collective_id=0, has_side_effects=True, vmem_limit_bytes=60 * 2**20),
    )(sky, col, rows, cnt, ws, live, codes, crd, jnp.asarray(dft_table()))


def solution(mesh):
    placed = (
        P("fy", "fx"), P(), P(), P("fx", "fy"), P("fx", "fy", None), P("fx", "fy"), P("fx", "fy", None),
        P("fx", "fy", None, None, None),
    )
    return jax.shard_map(
        per_device, mesh=mesh, in_specs=placed, out_specs=P("fx", "fy", None, None, None), check_vma=False
    )
```

```python
import functools

import jax
import jax.numpy as jnp
import numpy as np
from jax import lax
from jax.experimental import pallas as pl
from jax.experimental.pallas import tpu as pltpu
from jax.sharding import PartitionSpec as P

MESH = pl.DeviceIdType.MESH
SG = 1024
NSKY = 65536
NB = 16
NV = 128
SG0 = 32
NX = 4
NZ = 8
NQ = 8
HALF = SG // 2
F32 = jnp.float32
BF16 = jnp.bfloat16
SIN = (3.141592502593994, -5.167698860168457, 2.5499982833862305, -0.59855055809021, 0.0807478204369545, -0.00608947454020381)
COS = (1.0, -4.93480110168457, 4.058694839477539, -1.3351584672927856, 0.23502980172634125, -0.025358984246850014, 0.0015939107397571206)


def cis(turns):
    near = turns - jnp.floor(turns + 0.5)
    y = near + near
    z = y * y
    sine = jnp.full_like(z, SIN[-1])
    for c in SIN[-2::-1]:
        sine = sine * z + c
    cosine = jnp.full_like(z, COS[-1])
    for c in COS[-2::-1]:
        cosine = cosine * z + c
    return cosine, sine * y


def dft_table():
    row = np.arange(NZ * 32)
    b = 128 * (row // 32) + 2 * (row % 16) + (row // 16) % 2
    angle = (b[:, None] * np.arange(SG)[None, :]) % SG * (2 * np.pi / SG)
    return np.concatenate([np.cos(angle), -np.sin(angle)], axis=1).astype(BF16)


def iota(shape, axis):
    return lax.broadcasted_iota(jnp.int32, shape, axis)


def kernel(
    sky_h, col_h, row_h, cnt_h, ws_h, live_h, codes_h, crd_h, tab_h, out,
    sky, tmp, tab, crd, col, rows, cnt, ws, live, codes, gath, spec, w8, tw, ybuf, part, got, strips, cross, lines, fine, vtab, wtab, form,
    load_sem, send1, recv1, send2, recv2, send3, recv3,
):
    fx, fy = lax.axis_index("fx"), lax.axis_index("fy")
    z, x = fx // NX, lax.rem(fx, NX)

    along_z = [(lax.rem(z + d, NZ) * NX + x, fy) for d in range(1, NZ)]
    along_x = [(z * NX + lax.rem(x + d, NX), fy) for d in range(1, NX)]
    along_q = [(fx, lax.rem(fy + d, NQ)) for d in range(1, NQ)]
    barrier = pltpu.get_barrier_semaphore()
    for peer in [along_z[d - 1] for d in (4, 3, 5, 2, 6, 1, 7)] + along_x + along_q:
        pl.semaphore_signal(barrier, inc=1, device_id=peer, device_id_type=MESH)

    pairs = [(sky_h, sky), (col_h, col), (row_h, rows), (cnt_h, cnt), (ws_h, ws), (live_h, live), (codes_h, codes), (crd_h, crd), (tab_h, tab)]
    loads = [pltpu.make_async_copy(a, b, load_sem.at[i]) for i, (a, b) in enumerate(pairs)]
    for load in loads:
        load.start()

    loads[0].wait()
    for j in range(16):
        tmp[4 * j : 4 * j + 4, :] = sky[:, 128 * j : 128 * j + 128]
    left = iota((16, 128), 1) < 64
    line = [tmp[pl.ds(i, 16, stride=4), :] for i in range(4)]
    turned = [pltpu.roll(a, 64, 1) for a in line]
    halves = []
    for i in (0, 2):
        low = jnp.where(left, line[i], turned[i + 1])
        high = jnp.where(left, turned[i], line[i + 1])
        halves.append(jnp.concatenate([low, high], axis=0))
    gath[z] = jnp.concatenate(halves, axis=1).astype(BF16)

    pl.semaphore_wait(barrier, len(along_z) + len(along_x) + len(along_q))

    def phase1(d, slot):
        return pltpu.make_async_remote_copy(
            src_ref=gath.at[slot], dst_ref=gath.at[slot], send_sem=send1.at[d], recv_sem=recv1.at[d],
            device_id=along_z[d - 1], device_id_type=MESH,
        )

    sent1 = [phase1(d, z) for d in (4, 3, 5, 2, 6, 1, 7)]
    for copy in sent1:
        copy.start()
    for load in loads[1:]:
        load.wait()

    kappa = iota((8, SG), 1)
    c0 = iota((8, SG), 0)

    def wave(off):
        return off + jnp.bitwise_and(kappa - off, SG - 1)

    for d in range(NX):
        k = wave(col[z * NX + lax.rem(x + d, NX)])
        cosine, sine = cis(jnp.bitwise_and(k * 8, NSKY - 1).astype(F32) * (1.0 / NSKY))
        w8[d, 0] = cosine
        w8[d, 1] = -sine
        cosine, sine = cis(jnp.bitwise_and(c0 * k + 2048 * x * kappa, NSKY - 1).astype(F32) * (1.0 / NSKY))
        tw[d, 0] = cosine
        tw[d, 1] = -sine

    side = iota((8, HALF), 1)
    high = 2 * (side // 128) + iota((8, HALF), 0) // 4 - 4
    for r in range(8):
        mixed = jnp.bitwise_and(r * high * jnp.bitwise_and(side, 127), 7)
        cosine, sine = cis(mixed.astype(F32) * 0.125)
        cross[r, 0] = cosine
        cross[r, 1] = sine

    r = iota((128, 64), 0)
    m = iota((128, 64), 1)
    q, i = jnp.bitwise_and(r, 63) // 8, jnp.bitwise_and(r, 3)
    turn = jnp.bitwise_and((q * (NSKY // NQ) + i) * (rows[fy] + jnp.bitwise_and(m, 31)), NSKY - 1)
    quarter = (m >= 32).astype(jnp.int32) - (r >= 64).astype(jnp.int32)
    wide = cis(quarter.astype(F32) * 0.25 - turn.astype(F32) * (1.0 / NSKY))[0].astype(BF16)

    count = cnt[0, 0]
    g = iota((NV, NV), 0)
    m = iota((SG0, NV), 0)
    odd = (jnp.bitwise_and(iota((64, NV), 0), 4) * 32).astype(F32)

    def depth_of(b):
        plane = lax.rem(codes[0, 0, b], count)
        depth = jnp.int32(0)
        for layer in range(8):
            depth = depth + jnp.where(layer <= plane, ws[0, 0, layer], 0)
        return depth

    def fill(b, carry):
        depth = depth_of(b)
        u = crd[0, 0, b, 0:1, :]
        v = crd[0, 0, b, 1:2, :]
        screen = jnp.bitwise_and(depth * (m - 16) * (m - 16), 2047).astype(F32) * (1.0 / 2048)
        wave_real, wave_imag = cis(m.astype(F32) * u + screen)
        both = jnp.concatenate([wave_real, wave_imag], axis=0).astype(BF16)
        turned = jnp.dot(wide, both, preferred_element_type=F32)
        cosine, sine = cis(256.0 * jnp.broadcast_to(v, (8, NV)))
        wtab[b, 0] = cosine
        wtab[b, 1] = sine
        form[b] = jnp.bitwise_and(depth, 7)
        cosine, sine = cis(odd * v)
        vtab[b, 0:64] = turned[:64] * cosine - turned[64:] * sine
        vtab[b, 64:128] = turned[:64] * sine + turned[64:] * cosine
        screen = jnp.bitwise_and(depth * g * g, 2047).astype(F32) * (1.0 / 2048)
        cosine, sine = cis(g.astype(F32) * v + screen)
        fine[b, 0:NV, 0:NV] = cosine.astype(BF16)
        fine[b, 0:NV, NV : 2 * NV] = sine.astype(BF16)
        fine[b, NV : 2 * NV, 0:NV] = (-sine).astype(BF16)
        fine[b, NV : 2 * NV, NV : 2 * NV] = cosine.astype(BF16)
        return carry

    lax.fori_loop(0, NB, fill, 0)

    for d in range(1, NZ):
        phase1(d, lax.rem(z + NZ - d, NZ)).wait_recv()

    sky_t = gath[...].reshape(NZ * 32, 256)
    spec[...] = lax.dot_general(sky_t, tab[...], (((0,), (0,)), ((), ())), preferred_element_type=F32)
    pick_row = iota((8, 64), 0)
    pick_col = iota((8, 64), 1)
    pick = jnp.where(
        (pick_col // 16 == jnp.bitwise_and(pick_row, 3)) & (jnp.bitwise_and(pick_col // 8, 1) == pick_row // 4), 1.0, 0.0
    ).astype(BF16)

    def phase2(d):
        return pltpu.make_async_remote_copy(
            src_ref=part.at[d], dst_ref=got.at[d], send_sem=send2.at[d], recv_sem=recv2.at[d],
            device_id=along_x[d - 1], device_id_type=MESH,
        )

    own = None
    for d in (2, 1, 3, 0):
        def facet_row(x0, carry):
            for lo in (0, HALF):
                cols = slice(lo, lo + HALF)
                wr, wi = w8[d, 0, :, cols], w8[d, 1, :, cols]

                def at(c1, plus):
                    return spec[pl.ds(pl.multiple_of(x0 * 64 + 8 * c1, 8), 8), lo + plus : lo + plus + HALF]

                ar, ai = at(7, 0), at(7, SG)
                for c1 in range(6, -1, -1):
                    ar, ai = ar * wr - ai * wi + at(c1, 0), ar * wi + ai * wr + at(c1, SG)
                tr, ti = tw[d, 0, :, cols], tw[d, 1, :, cols]
                both = jnp.concatenate([ar * tr - ai * ti, ar * ti + ai * tr], axis=0)
                ybuf[d, pl.ds(pl.multiple_of(x0 * 16, 16), 16), cols] = both.astype(BF16)
            return carry

        lax.fori_loop(0, 4, facet_row, 0)
        strip = jnp.dot(pick, ybuf[d], preferred_element_type=F32)
        packed = jnp.concatenate([strip[:, :HALF], strip[:, HALF:]], axis=0)
        if d:
            part[d] = packed.astype(BF16)
            phase2(d).start()
        else:
            own = packed
    for d in (1, 3, 2):
        phase2(d).wait_recv()
        own = own + got[d].astype(F32)

    flat = jnp.concatenate([own[:8], own[8:]], axis=1)
    flat = pltpu.roll(flat, jnp.bitwise_and(SG - jnp.bitwise_and(col[fx], SG - 1), SG - 1), 1)
    upper = iota((8, 128), 0) < 4
    real, imag = [], []
    for hh in range(4):
        even, odd_h = flat[:, 256 * hh : 256 * hh + 128], flat[:, 256 * hh + 128 : 256 * hh + 256]
        real.append(jnp.where(upper, even, pltpu.roll(odd_h, 4, 0)))
        imag.append(jnp.where(upper, pltpu.roll(even, 4, 0), odd_h))
    packed = jnp.concatenate([jnp.concatenate(real, axis=1), jnp.concatenate(imag, axis=1)], axis=0)
    strips[fy] = packed.astype(BF16)

    def phase3(d, slot):
        return pltpu.make_async_remote_copy(
            src_ref=strips.at[slot], dst_ref=strips.at[slot], send_sem=send3.at[d], recv_sem=recv3.at[d],
            device_id=along_q[d - 1], device_id_type=MESH,
        )

    sent3 = [phase3(d, fy) for d in (4, 3, 5, 2, 6, 1, 7)]
    for copy in sent3:
        copy.start()
    for d in range(1, NQ):
        phase3(d, lax.rem(fy + NQ - d, NQ)).wait_recv()
    for hh in range(4):
        cols = slice(128 * hh, 128 * hh + 128)
        block = strips[:, :, cols].astype(F32)
        real, imag = block[:, 0:8, :], block[:, 8:16, :]
        for r in range(8):
            cosine, sine = cross[r, 0:1, :, cols], cross[r, 1:2, :, cols]
            lines[r, 64 * hh : 64 * hh + 64, 0:128] = (real * cosine - imag * sine).reshape(64, 128).astype(BF16)
            lines[r, 64 * hh : 64 * hh + 64, 128:256] = (real * sine + imag * cosine).reshape(64, 128).astype(BF16)

    def degrid(b, carry):
        prod = jnp.dot(lines[form[b]], fine[b], preferred_element_type=F32)
        wr, wi = wtab[b, 0:1], wtab[b, 1:2]

        def tile(hh, lo):
            return prod[64 * hh : 64 * hh + 64, lo : lo + NV].reshape(8, 8, NV)

        ar, ai = tile(3, 0), tile(3, NV)
        for hh in (2, 1, 0):
            ar, ai = ar * wr - ai * wi + tile(hh, 0), ar * wi + ai * wr + tile(hh, NV)
        vr, vi = vtab[b, 0:64].reshape(8, 8, NV), vtab[b, 64:128].reshape(8, 8, NV)
        scale = jnp.where(b < live[0, 0], 2.0**-18, 0.0)
        real = jnp.sum(vr * ar - vi * ai, axis=0)
        imag = jnp.sum(vr * ai + vi * ar, axis=0)
        out[0, 0, b, 0:1, :] = jnp.sum(real, axis=0, keepdims=True) * scale
        out[0, 0, b, 1:2, :] = jnp.sum(imag, axis=0, keepdims=True) * scale
        return carry

    lax.fori_loop(0, NB, degrid, 0, unroll=16)

    for copy in sent1:
        copy.wait_send()
    for d in (2, 1, 3):
        phase2(d).wait_send()
    for copy in sent3:
        copy.wait_send()


def per_device(sky, col, rows, cnt, ws, live, codes, crd):
    hbm = pl.BlockSpec(memory_space=pl.ANY)
    dma = pltpu.SemaphoreType.DMA
    return pl.pallas_call(
        kernel,
        out_shape=jax.ShapeDtypeStruct((1, 1, NB, 2, NV), F32),
        in_specs=[hbm] * 9,
        out_specs=pl.BlockSpec(memory_space=pltpu.VMEM),
        scratch_shapes=[
            pltpu.VMEM((4, 2048), F32),
            pltpu.VMEM((64, 128), F32),
            pltpu.VMEM((256, 2 * SG), BF16),
            pltpu.VMEM((1, 1, NB, 2, NV), F32),
            pltpu.SMEM((32,), jnp.int32),
            pltpu.SMEM((8,), jnp.int32),
            pltpu.SMEM((1, 1), jnp.int32),
            pltpu.SMEM((1, 1, 8), jnp.int32),
            pltpu.SMEM((1, 1), jnp.int32),
            pltpu.SMEM((1, 1, NB), jnp.int32),
            pltpu.VMEM((NZ, 32, 256), BF16),
            pltpu.VMEM((256, 2 * SG), F32),
            pltpu.VMEM((NX, 2, 8, SG), F32),
            pltpu.VMEM((NX, 2, 8, SG), F32),
            pltpu.VMEM((NX, 64, SG), BF16),
            pltpu.VMEM((NX, 16, HALF), BF16),
            pltpu.VMEM((NX, 16, HALF), BF16),
            pltpu.VMEM((NQ, 16, HALF), BF16),
            pltpu.VMEM((8, 2, 8, HALF), F32),
            pltpu.VMEM((8, 256, 256), BF16),
            pltpu.VMEM((NB, 2 * NV, 2 * NV), BF16),
            pltpu.VMEM((NB, 128, NV), F32),
            pltpu.VMEM((NB, 2, 8, NV), F32),
            pltpu.SMEM((NB,), jnp.int32),
            dma((9,)), dma((NZ,)), dma((NZ,)), dma((NX,)), dma((NX,)), dma((NQ,)), dma((NQ,)),
        ],
        compiler_params=pltpu.CompilerParams(collective_id=0, has_side_effects=True, vmem_limit_bytes=60 * 2**20),
    )(sky, col, rows, cnt, ws, live, codes, crd, jnp.asarray(dft_table()))


def solution(mesh):
    placed = (
        P("fy", "fx"), P(), P(), P("fx", "fy"), P("fx", "fy", None), P("fx", "fy"), P("fx", "fy", None),
        P("fx", "fy", None, None, None),
    )
    return jax.shard_map(
        per_device, mesh=mesh, in_specs=placed, out_specs=P("fx", "fy", None, None, None), check_vma=False
    )
```

```python
import functools

import jax
import jax.numpy as jnp
import numpy as np
from jax import lax
from jax.experimental import pallas as pl
from jax.experimental.pallas import tpu as pltpu
from jax.sharding import PartitionSpec as P

MESH = pl.DeviceIdType.MESH
SG = 1024
NSKY = 65536
NB = 16
NV = 128
SG0 = 32
NX = 4
NZ = 8
NY = 4
NQ = 8
HALF = SG // 2
F32 = jnp.float32
BF16 = jnp.bfloat16
SIN = (3.141592502593994, -5.167698860168457, 2.5499982833862305, -0.59855055809021, 0.0807478204369545, -0.00608947454020381)
COS = (1.0, -4.93480110168457, 4.058694839477539, -1.3351584672927856, 0.23502980172634125, -0.025358984246850014, 0.0015939107397571206)


def cis(turns):
    near = turns - jnp.floor(turns + 0.5)
    y = near + near
    z = y * y
    sine = jnp.full_like(z, SIN[-1])
    for c in SIN[-2::-1]:
        sine = sine * z + c
    cosine = jnp.full_like(z, COS[-1])
    for c in COS[-2::-1]:
        cosine = cosine * z + c
    return cosine, sine * y


def dft_table():
    row = np.arange(NZ * 32)
    b = 128 * (row // 32) + 2 * (row % 16) + (row // 16) % 2
    angle = (b[:, None] * np.arange(SG)[None, :]) % SG * (2 * np.pi / SG)
    return np.concatenate([np.cos(angle), -np.sin(angle)], axis=1).astype(BF16)


def iota(shape, axis):
    return lax.broadcasted_iota(jnp.int32, shape, axis)


def kernel(
    sky_h, col_h, row_h, cnt_h, ws_h, live_h, codes_h, crd_h, tab_h, out,
    sky, tmp, tab, crd, col, rows, cnt, ws, live, codes, gath, spec, w8, tw, ybuf, part, got, strips, cross, lines, fine, vtab, wtab, form,
    load_sem, send1, recv1, send2, recv2, send3, recv3,
):
    fx, fy = lax.axis_index("fx"), lax.axis_index("fy")
    z, x = fx // NX, lax.rem(fx, NX)
    y, core = fy // 2, lax.rem(fy, 2)

    along_z = [(lax.rem(z + d, NZ) * NX + x, fy) for d in range(1, NZ)]
    plane = {
        (dx, dy): (z * NX + lax.rem(x + dx, NX), lax.rem(y + dy, NY) * 2 + core)
        for dx in (2, 1, 3, 0) for dy in (2, 1, 3, 0) if dx or dy
    }
    other = (fx, y * 2 + 1 - core)
    peers = [along_z[d - 1] for d in (4, 3, 5, 2, 6, 1, 7)] + list(plane.values()) + [other]
    barrier = pltpu.get_barrier_semaphore()
    for peer in peers:
        pl.semaphore_signal(barrier, inc=1, device_id=peer, device_id_type=MESH)

    pairs = [(sky_h, sky), (col_h, col), (row_h, rows), (cnt_h, cnt), (ws_h, ws), (live_h, live), (codes_h, codes), (crd_h, crd), (tab_h, tab)]
    loads = [pltpu.make_async_copy(a, b, load_sem.at[i]) for i, (a, b) in enumerate(pairs)]
    for load in loads:
        load.start()

    loads[0].wait()
    for j in range(16):
        tmp[4 * j : 4 * j + 4, :] = sky[:, 128 * j : 128 * j + 128]
    left = iota((16, 128), 1) < 64
    line = [tmp[pl.ds(i, 16, stride=4), :] for i in range(4)]
    turned = [pltpu.roll(a, 64, 1) for a in line]
    halves = []
    for i in (0, 2):
        low = jnp.where(left, line[i], turned[i + 1])
        high = jnp.where(left, turned[i], line[i + 1])
        halves.append(jnp.concatenate([low, high], axis=0))
    gath[z] = jnp.concatenate(halves, axis=1).astype(BF16)

    pl.semaphore_wait(barrier, len(peers))

    def phase1(slot, there):
        return pltpu.make_async_remote_copy(
            src_ref=gath.at[slot], dst_ref=gath.at[slot], send_sem=send1.at[there], recv_sem=recv1.at[slot],
            device_id=(there * NX + x, fy), device_id_type=MESH,
        )

    others_z = [j + (z <= j).astype(jnp.int32) for j in range(NZ - 1)]
    sent1 = [phase1(z, there) for there in others_z]
    for copy in sent1:
        copy.start()
    for load in loads[1:]:
        load.wait()

    kappa = iota((8, SG), 1)
    c0 = iota((8, SG), 0)

    def wave(off):
        return off + jnp.bitwise_and(kappa - off, SG - 1)

    for d in range(NX):
        k = wave(col[z * NX + d])
        cosine, sine = cis(jnp.bitwise_and(k * 8, NSKY - 1).astype(F32) * (1.0 / NSKY))
        w8[d, 0] = cosine
        w8[d, 1] = -sine
        cosine, sine = cis(jnp.bitwise_and(c0 * k + 2048 * x * kappa, NSKY - 1).astype(F32) * (1.0 / NSKY))
        tw[d, 0] = cosine
        tw[d, 1] = -sine

    side = iota((8, HALF), 1)
    high = 2 * (side // 128) + iota((8, HALF), 0) // 4 - 4
    for r in range(8):
        mixed = jnp.bitwise_and(r * high * jnp.bitwise_and(side, 127), 7)
        cosine, sine = cis(mixed.astype(F32) * 0.125)
        cross[r, 0] = cosine
        cross[r, 1] = sine

    r = iota((128, 64), 0)
    m = iota((128, 64), 1)
    q = 2 * (jnp.bitwise_and(r, 31) // 8) + jnp.bitwise_and(r, 63) // 32
    i = jnp.bitwise_and(r, 3)
    turn = jnp.bitwise_and((q * (NSKY // NQ) + i) * (rows[fy] + jnp.bitwise_and(m, 31)), NSKY - 1)
    quarter = (m >= 32).astype(jnp.int32) - (r >= 64).astype(jnp.int32)
    wide = cis(quarter.astype(F32) * 0.25 - turn.astype(F32) * (1.0 / NSKY))[0].astype(BF16)

    count = cnt[0, 0]
    g = iota((NV, NV), 0)
    m = iota((SG0, NV), 0)
    odd = (jnp.bitwise_and(iota((64, NV), 0), 4) * 32).astype(F32)

    def depth_of(b):
        plane = lax.rem(codes[0, 0, b], count)
        depth = jnp.int32(0)
        for layer in range(8):
            depth = depth + jnp.where(layer <= plane, ws[0, 0, layer], 0)
        return depth

    def fill(b, carry):
        depth = depth_of(b)
        u = crd[0, 0, b, 0:1, :]
        v = crd[0, 0, b, 1:2, :]
        screen = jnp.bitwise_and(depth * (m - 16) * (m - 16), 2047).astype(F32) * (1.0 / 2048)
        wave_real, wave_imag = cis(m.astype(F32) * u + screen)
        both = jnp.concatenate([wave_real, wave_imag], axis=0).astype(BF16)
        turned = jnp.dot(wide, both, preferred_element_type=F32)
        cosine, sine = cis(256.0 * jnp.broadcast_to(v, (8, NV)))
        wtab[b, 0] = cosine
        wtab[b, 1] = sine
        form[b] = jnp.bitwise_and(depth, 7)
        cosine, sine = cis(odd * v)
        vtab[b, 0:64] = turned[:64] * cosine - turned[64:] * sine
        vtab[b, 64:128] = turned[:64] * sine + turned[64:] * cosine
        screen = jnp.bitwise_and(depth * g * g, 2047).astype(F32) * (1.0 / 2048)
        cosine, sine = cis(g.astype(F32) * v + screen)
        fine[b, 0:NV, 0:NV] = cosine.astype(BF16)
        fine[b, 0:NV, NV : 2 * NV] = sine.astype(BF16)
        fine[b, NV : 2 * NV, 0:NV] = (-sine).astype(BF16)
        fine[b, NV : 2 * NV, NV : 2 * NV] = cosine.astype(BF16)
        return carry

    lax.fori_loop(0, NB, fill, 0)

    for there in others_z:
        phase1(there, there).wait_recv()

    sky_t = gath[...].reshape(NZ * 32, 256)
    spec[...] = lax.dot_general(sky_t, tab[...], (((0,), (0,)), ((), ())), preferred_element_type=F32)
    pick_row = iota((8, 64), 0)
    pick_col = iota((8, 64), 1)
    pick = jnp.where(
        (pick_col // 16 == jnp.bitwise_and(pick_row, 3)) & (jnp.bitwise_and(pick_col // 8, 1) == pick_row // 4), 1.0, 0.0
    ).astype(BF16)

    def phase2(slot, to_x, to_y):
        return pltpu.make_async_remote_copy(
            src_ref=part.at[to_x], dst_ref=got.at[slot], send_sem=send2.at[NY * to_x + to_y], recv_sem=recv2.at[slot],
            device_id=(z * NX + to_x, to_y * 2 + core), device_id_type=MESH,
        )

    here = NY * x + y
    others_xy = [j + (here <= j).astype(jnp.int32) for j in range(NX * NY - 1)]
    for d in range(NX):
        def facet_row(x0, carry):
            for lo in (0, HALF):
                cols = slice(lo, lo + HALF)
                wr, wi = w8[d, 0, :, cols], w8[d, 1, :, cols]

                def at(c1, plus):
                    return spec[pl.ds(pl.multiple_of(x0 * 64 + 8 * c1, 8), 8), lo + plus : lo + plus + HALF]

                ar, ai = at(7, 0), at(7, SG)
                for c1 in range(6, -1, -1):
                    ar, ai = ar * wr - ai * wi + at(c1, 0), ar * wi + ai * wr + at(c1, SG)
                tr, ti = tw[d, 0, :, cols], tw[d, 1, :, cols]
                both = jnp.concatenate([ar * tr - ai * ti, ar * ti + ai * tr], axis=0)
                ybuf[d, pl.ds(pl.multiple_of(x0 * 16, 16), 16), cols] = both.astype(BF16)
            return carry

        lax.fori_loop(0, 4, facet_row, 0)
        strip = jnp.dot(pick, ybuf[d], preferred_element_type=F32)
        packed = jnp.concatenate([strip[:, :HALF], strip[:, HALF:]], axis=0)
        part[d] = packed.astype(BF16)
        for to_y in range(NY):
            @pl.when(jnp.logical_or(x != d, y != to_y))
            def send():
                phase2(here, d, to_y).start()

    got[here] = part[x]
    for there in others_xy:
        phase2(there, there // NY, lax.rem(there, NY)).wait_recv()

    totals = []
    for dy in range(NY):
        total = got[dy].astype(F32)
        for dx in range(1, NX):
            total = total + got[NY * dx + dy].astype(F32)
        totals.append(jnp.concatenate([total[:8], total[8:]], axis=1))
    shift = jnp.bitwise_and(SG - jnp.bitwise_and(col[fx], SG - 1), SG - 1)
    ordered = pltpu.roll(jnp.concatenate(totals, axis=0), shift, 1)
    upper = iota((8, 128), 0) < 4
    for dy in range(NY):
        flat = ordered[8 * dy : 8 * dy + 8]
        real, imag = [], []
        for hh in range(4):
            even, odd_h = flat[:, 256 * hh : 256 * hh + 128], flat[:, 256 * hh + 128 : 256 * hh + 256]
            real.append(jnp.where(upper, even, pltpu.roll(odd_h, 4, 0)))
            imag.append(jnp.where(upper, pltpu.roll(even, 4, 0), odd_h))
        packed = jnp.concatenate([jnp.concatenate(real, axis=1), jnp.concatenate(imag, axis=1)], axis=0)
        strips[core, dy] = packed.astype(BF16)

    def phase3(slot):
        return pltpu.make_async_remote_copy(
            src_ref=strips.at[slot], dst_ref=strips.at[slot], send_sem=send3, recv_sem=recv3,
            device_id=other, device_id_type=MESH,
        )

    sent3 = phase3(core)
    sent3.start()
    phase3(1 - core).wait_recv()
    for hh in range(4):
        cols = slice(128 * hh, 128 * hh + 128)
        block = strips[:, :, :, cols].astype(F32).reshape(NQ, 16, 128)
        real, imag = block[:, 0:8, :], block[:, 8:16, :]
        for r in range(8):
            cosine, sine = cross[r, 0:1, :, cols], cross[r, 1:2, :, cols]
            lines[r, 64 * hh : 64 * hh + 64, 0:128] = (real * cosine - imag * sine).reshape(64, 128).astype(BF16)
            lines[r, 64 * hh : 64 * hh + 64, 128:256] = (real * sine + imag * cosine).reshape(64, 128).astype(BF16)

    def degrid(b, carry):
        prod = jnp.dot(lines[form[b]], fine[b], preferred_element_type=F32)
        wr, wi = wtab[b, 0:1], wtab[b, 1:2]

        def tile(hh, lo):
            return prod[64 * hh : 64 * hh + 64, lo : lo + NV].reshape(8, 8, NV)

        ar, ai = tile(3, 0), tile(3, NV)
        for hh in (2, 1, 0):
            ar, ai = ar * wr - ai * wi + tile(hh, 0), ar * wi + ai * wr + tile(hh, NV)
        vr, vi = vtab[b, 0:64].reshape(8, 8, NV), vtab[b, 64:128].reshape(8, 8, NV)
        scale = jnp.where(b < live[0, 0], 2.0**-18, 0.0)
        real = jnp.sum(vr * ar - vi * ai, axis=0)
        imag = jnp.sum(vr * ai + vi * ar, axis=0)
        out[0, 0, b, 0:1, :] = jnp.sum(real, axis=0, keepdims=True) * scale
        out[0, 0, b, 1:2, :] = jnp.sum(imag, axis=0, keepdims=True) * scale
        return carry

    lax.fori_loop(0, NB, degrid, 0, unroll=16)

    for copy in sent1:
        copy.wait_send()
    for there in others_xy:
        phase2(here, there // NY, lax.rem(there, NY)).wait_send()
    sent3.wait_send()


def per_device(sky, col, rows, cnt, ws, live, codes, crd):
    hbm = pl.BlockSpec(memory_space=pl.ANY)
    dma = pltpu.SemaphoreType.DMA
    return pl.pallas_call(
        kernel,
        out_shape=jax.ShapeDtypeStruct((1, 1, NB, 2, NV), F32),
        in_specs=[hbm] * 9,
        out_specs=pl.BlockSpec(memory_space=pltpu.VMEM),
        scratch_shapes=[
            pltpu.VMEM((4, 2048), F32),
            pltpu.VMEM((64, 128), F32),
            pltpu.VMEM((256, 2 * SG), BF16),
            pltpu.VMEM((1, 1, NB, 2, NV), F32),
            pltpu.SMEM((32,), jnp.int32),
            pltpu.SMEM((8,), jnp.int32),
            pltpu.SMEM((1, 1), jnp.int32),
            pltpu.SMEM((1, 1, 8), jnp.int32),
            pltpu.SMEM((1, 1), jnp.int32),
            pltpu.SMEM((1, 1, NB), jnp.int32),
            pltpu.VMEM((NZ, 32, 256), BF16),
            pltpu.VMEM((256, 2 * SG), F32),
            pltpu.VMEM((NX, 2, 8, SG), F32),
            pltpu.VMEM((NX, 2, 8, SG), F32),
            pltpu.VMEM((NX, 64, SG), BF16),
            pltpu.VMEM((NX, 16, HALF), BF16),
            pltpu.VMEM((NX * NY, 16, HALF), BF16),
            pltpu.VMEM((2, NY, 16, HALF), BF16),
            pltpu.VMEM((8, 2, 8, HALF), F32),
            pltpu.VMEM((8, 256, 256), BF16),
            pltpu.VMEM((NB, 2 * NV, 2 * NV), BF16),
            pltpu.VMEM((NB, 128, NV), F32),
            pltpu.VMEM((NB, 2, 8, NV), F32),
            pltpu.SMEM((NB,), jnp.int32),
            dma((9,)), dma((NZ,)), dma((NZ,)), dma((NX * NY,)), dma((NX * NY,)), dma, dma,
        ],
        compiler_params=pltpu.CompilerParams(collective_id=0, has_side_effects=True, vmem_limit_bytes=60 * 2**20),
    )(sky, col, rows, cnt, ws, live, codes, crd, jnp.asarray(dft_table()))


def solution(mesh):
    placed = (
        P("fy", "fx"), P(), P(), P("fx", "fy"), P("fx", "fy", None), P("fx", "fy"), P("fx", "fy", None),
        P("fx", "fy", None, None, None),
    )
    return jax.shard_map(
        per_device, mesh=mesh, in_specs=placed, out_specs=P("fx", "fy", None, None, None), check_vma=False
    )
```

```python
import functools

import jax
import jax.numpy as jnp
import numpy as np
from jax import lax
from jax.experimental import pallas as pl
from jax.experimental.pallas import tpu as pltpu
from jax.sharding import PartitionSpec as P

MESH = pl.DeviceIdType.MESH
SG = 1024
NSKY = 65536
NB = 16
NV = 128
SG0 = 32
NX = 4
NZ = 8
NY = 4
NQ = 8
HALF = SG // 2
F32 = jnp.float32
BF16 = jnp.bfloat16
SIN = (3.141592502593994, -5.167698860168457, 2.5499982833862305, -0.59855055809021, 0.0807478204369545, -0.00608947454020381)
COS = (1.0, -4.93480110168457, 4.058694839477539, -1.3351584672927856, 0.23502980172634125, -0.025358984246850014, 0.0015939107397571206)


def cis(turns):
    near = turns - jnp.floor(turns + 0.5)
    y = near + near
    z = y * y
    sine = jnp.full_like(z, SIN[-1])
    for c in SIN[-2::-1]:
        sine = sine * z + c
    cosine = jnp.full_like(z, COS[-1])
    for c in COS[-2::-1]:
        cosine = cosine * z + c
    return cosine, sine * y


def dft_table():
    row = np.arange(NZ * 32)
    b = 128 * (row // 32) + 2 * (row % 16) + (row // 16) % 2
    angle = (b[:, None] * np.arange(SG)[None, :]) % SG * (2 * np.pi / SG)
    return np.concatenate([np.cos(angle), -np.sin(angle)], axis=1).astype(BF16)


def iota(shape, axis):
    return lax.broadcasted_iota(jnp.int32, shape, axis)


def kernel(
    sky_h, col_h, row_h, cnt_h, ws_h, live_h, codes_h, crd_h, tab_h, out,
    sky, tmp, tab, crd, col, rows, cnt, ws, live, codes, gath, spec, w8, tw, ybuf, part, got, strips, cross, lines, fine, vtab, wtab, form, acc,
    load_sem, send1, recv1, send2, recv2, send3, recv3,
):
    fx, fy = lax.axis_index("fx"), lax.axis_index("fy")
    z, x = fx // NX, lax.rem(fx, NX)
    y, core = fy // 2, lax.rem(fy, 2)

    along_z = [(lax.rem(z + d, NZ) * NX + x, fy) for d in range(1, NZ)]
    plane = {
        (dx, dy): (z * NX + lax.rem(x + dx, NX), lax.rem(y + dy, NY) * 2 + core)
        for dx in (2, 1, 3, 0) for dy in (2, 1, 3, 0) if dx or dy
    }
    other = (fx, y * 2 + 1 - core)
    peers = [along_z[d - 1] for d in (4, 3, 5, 2, 6, 1, 7)] + list(plane.values()) + [other]
    barrier = pltpu.get_barrier_semaphore()
    for peer in peers:
        pl.semaphore_signal(barrier, inc=1, device_id=peer, device_id_type=MESH)

    pairs = [(sky_h, sky), (col_h, col), (row_h, rows), (cnt_h, cnt), (ws_h, ws), (live_h, live), (codes_h, codes), (crd_h, crd), (tab_h, tab)]
    loads = [pltpu.make_async_copy(a, b, load_sem.at[i]) for i, (a, b) in enumerate(pairs)]
    for load in loads:
        load.start()

    loads[0].wait()
    for j in range(16):
        tmp[4 * j : 4 * j + 4, :] = sky[:, 128 * j : 128 * j + 128]
    left = iota((16, 128), 1) < 64
    line = [tmp[pl.ds(i, 16, stride=4), :] for i in range(4)]
    turned = [pltpu.roll(a, 64, 1) for a in line]
    halves = []
    for i in (0, 2):
        low = jnp.where(left, line[i], turned[i + 1])
        high = jnp.where(left, turned[i], line[i + 1])
        halves.append(jnp.concatenate([low, high], axis=0))
    gath[z] = jnp.concatenate(halves, axis=1).astype(BF16)

    pl.semaphore_wait(barrier, len(peers))

    def phase1(slot, there):
        return pltpu.make_async_remote_copy(
            src_ref=gath.at[slot], dst_ref=gath.at[slot], send_sem=send1.at[there], recv_sem=recv1.at[slot],
            device_id=(there * NX + x, fy), device_id_type=MESH,
        )

    others_z = [j + (z <= j).astype(jnp.int32) for j in range(NZ - 1)]
    sent1 = [phase1(z, there) for there in others_z]
    for copy in sent1:
        copy.start()
    for load in loads[1:]:
        load.wait()

    kappa = iota((8, SG), 1)
    c0 = iota((8, SG), 0)

    def wave(off):
        return off + jnp.bitwise_and(kappa - off, SG - 1)

    for d in range(NX):
        k = wave(col[z * NX + d])
        cosine, sine = cis(jnp.bitwise_and(k * 8, NSKY - 1).astype(F32) * (1.0 / NSKY))
        w8[d, 0] = cosine
        w8[d, 1] = -sine
        cosine, sine = cis(jnp.bitwise_and(c0 * k + 2048 * x * kappa, NSKY - 1).astype(F32) * (1.0 / NSKY))
        tw[d, 0] = cosine
        tw[d, 1] = -sine

    side = iota((8, HALF), 1)
    high = 2 * (side // 128) + iota((8, HALF), 0) // 4 - 4
    for r in range(8):
        mixed = jnp.bitwise_and(r * high * jnp.bitwise_and(side, 127), 7)
        cosine, sine = cis(mixed.astype(F32) * 0.125)
        cross[r, 0] = cosine
        cross[r, 1] = sine

    r = iota((128, 64), 0)
    m = iota((128, 64), 1)
    q = 2 * (jnp.bitwise_and(r, 31) // 8) + jnp.where(jnp.bitwise_and(r, 32) == 0, core, 1 - core)
    i = jnp.bitwise_and(r, 3)
    turn = jnp.bitwise_and((q * (NSKY // NQ) + i) * (rows[fy] + jnp.bitwise_and(m, 31)), NSKY - 1)
    quarter = (m >= 32).astype(jnp.int32) - (r >= 64).astype(jnp.int32)
    wide = cis(quarter.astype(F32) * 0.25 - turn.astype(F32) * (1.0 / NSKY))[0].astype(BF16)

    count = cnt[0, 0]
    g = iota((NV, NV), 0)
    m = iota((SG0, NV), 0)
    odd = (jnp.bitwise_and(iota((64, NV), 0), 4) * 32).astype(F32)

    def depth_of(b):
        plane = lax.rem(codes[0, 0, b], count)
        depth = jnp.int32(0)
        for layer in range(8):
            depth = depth + jnp.where(layer <= plane, ws[0, 0, layer], 0)
        return depth

    def fill(b, carry):
        depth = depth_of(b)
        u = crd[0, 0, b, 0:1, :]
        v = crd[0, 0, b, 1:2, :]
        screen = jnp.bitwise_and(depth * (m - 16) * (m - 16), 2047).astype(F32) * (1.0 / 2048)
        wave_real, wave_imag = cis(m.astype(F32) * u + screen)
        both = jnp.concatenate([wave_real, wave_imag], axis=0).astype(BF16)
        turned = jnp.dot(wide, both, preferred_element_type=F32)
        cosine, sine = cis(256.0 * jnp.broadcast_to(v, (8, NV)))
        wtab[b, 0] = cosine
        wtab[b, 1] = sine
        form[b] = jnp.bitwise_and(depth, 7)
        cosine, sine = cis(odd * v)
        vtab[b, 0:64] = turned[:64] * cosine - turned[64:] * sine
        vtab[b, 64:128] = turned[:64] * sine + turned[64:] * cosine
        screen = jnp.bitwise_and(depth * g * g, 2047).astype(F32) * (1.0 / 2048)
        cosine, sine = cis(g.astype(F32) * v + screen)
        fine[b, 0:NV, 0:NV] = cosine.astype(BF16)
        fine[b, 0:NV, NV : 2 * NV] = sine.astype(BF16)
        fine[b, NV : 2 * NV, 0:NV] = (-sine).astype(BF16)
        fine[b, NV : 2 * NV, NV : 2 * NV] = cosine.astype(BF16)
        return carry

    lax.fori_loop(0, NB, fill, 0)

    for there in others_z:
        phase1(there, there).wait_recv()

    sky_t = gath[...].reshape(NZ * 32, 256)
    spec[...] = lax.dot_general(sky_t, tab[...], (((0,), (0,)), ((), ())), preferred_element_type=F32)
    pick_row = iota((8, 64), 0)
    pick_col = iota((8, 64), 1)
    pick = jnp.where(
        (pick_col // 16 == jnp.bitwise_and(pick_row, 3)) & (jnp.bitwise_and(pick_col // 8, 1) == pick_row // 4), 1.0, 0.0
    ).astype(BF16)

    def phase2(slot, to_x, to_y):
        return pltpu.make_async_remote_copy(
            src_ref=part.at[to_x], dst_ref=got.at[slot], send_sem=send2.at[NY * to_x + to_y], recv_sem=recv2.at[slot],
            device_id=(z * NX + to_x, to_y * 2 + core), device_id_type=MESH,
        )

    here = NY * x + y
    others_xy = [j + (here <= j).astype(jnp.int32) for j in range(NX * NY - 1)]
    for d in range(NX):
        def facet_row(x0, carry):
            for lo in (0, HALF):
                cols = slice(lo, lo + HALF)
                wr, wi = w8[d, 0, :, cols], w8[d, 1, :, cols]

                def at(c1, plus):
                    return spec[pl.ds(pl.multiple_of(x0 * 64 + 8 * c1, 8), 8), lo + plus : lo + plus + HALF]

                ar, ai = at(7, 0), at(7, SG)
                for c1 in range(6, -1, -1):
                    ar, ai = ar * wr - ai * wi + at(c1, 0), ar * wi + ai * wr + at(c1, SG)
                tr, ti = tw[d, 0, :, cols], tw[d, 1, :, cols]
                both = jnp.concatenate([ar * tr - ai * ti, ar * ti + ai * tr], axis=0)
                ybuf[d, pl.ds(pl.multiple_of(x0 * 16, 16), 16), cols] = both.astype(BF16)
            return carry

        lax.fori_loop(0, 4, facet_row, 0)
        strip = jnp.dot(pick, ybuf[d], preferred_element_type=F32)
        packed = jnp.concatenate([strip[:, :HALF], strip[:, HALF:]], axis=0)
        part[d] = packed.astype(BF16)
        for to_y in range(NY):
            @pl.when(jnp.logical_or(x != d, y != to_y))
            def send():
                phase2(here, d, to_y).start()

    got[here] = part[x]
    for there in others_xy:
        phase2(there, there // NY, lax.rem(there, NY)).wait_recv()

    totals = []
    for dy in range(NY):
        total = got[dy].astype(F32)
        for dx in range(1, NX):
            total = total + got[NY * dx + dy].astype(F32)
        totals.append(jnp.concatenate([total[:8], total[8:]], axis=1))
    shift = jnp.bitwise_and(SG - jnp.bitwise_and(col[fx], SG - 1), SG - 1)
    ordered = pltpu.roll(jnp.concatenate(totals, axis=0), shift, 1)
    upper = iota((8, 128), 0) < 4
    for dy in range(NY):
        flat = ordered[8 * dy : 8 * dy + 8]
        real, imag = [], []
        for hh in range(4):
            even, odd_h = flat[:, 256 * hh : 256 * hh + 128], flat[:, 256 * hh + 128 : 256 * hh + 256]
            real.append(jnp.where(upper, even, pltpu.roll(odd_h, 4, 0)))
            imag.append(jnp.where(upper, pltpu.roll(even, 4, 0), odd_h))
        packed = jnp.concatenate([jnp.concatenate(real, axis=1), jnp.concatenate(imag, axis=1)], axis=0)
        strips[core, dy] = packed.astype(BF16)

    def phase3(slot):
        return pltpu.make_async_remote_copy(
            src_ref=strips.at[slot], dst_ref=strips.at[slot], send_sem=send3, recv_sem=recv3,
            device_id=other, device_id_type=MESH,
        )

    sent3 = phase3(core)
    sent3.start()

    def turn_lines(where, half):
        for hh in range(4):
            cols = slice(128 * hh, 128 * hh + 128)
            rows_at = slice(32 * hh, 32 * hh + 32)
            block = strips[where, :, :, cols].astype(F32)
            real, imag = block[:, 0:8, :], block[:, 8:16, :]
            for r in range(8):
                cosine, sine = cross[r, 0:1, :, cols], cross[r, 1:2, :, cols]
                lines[r, half, rows_at, 0:128] = (real * cosine - imag * sine).reshape(32, 128).astype(BF16)
                lines[r, half, rows_at, 128:256] = (real * sine + imag * cosine).reshape(32, 128).astype(BF16)

    def gridded(b, half):
        prod = jnp.dot(lines[form[b], half], fine[b], preferred_element_type=F32)
        wr, wi = wtab[b, 0:1], wtab[b, 1:2]

        def tile(hh, lo):
            return prod[32 * hh : 32 * hh + 32, lo : lo + NV].reshape(4, 8, NV)

        ar, ai = tile(3, 0), tile(3, NV)
        for hh in (2, 1, 0):
            ar, ai = ar * wr - ai * wi + tile(hh, 0), ar * wi + ai * wr + tile(hh, NV)
        at = 32 * half
        vr, vi = vtab[b, at : at + 32].reshape(4, 8, NV), vtab[b, 64 + at : 96 + at].reshape(4, 8, NV)
        return jnp.sum(vr * ar - vi * ai, axis=0), jnp.sum(vr * ai + vi * ar, axis=0)

    def own_rows(b, carry):
        acc[b, 0], acc[b, 1] = gridded(b, 0)
        return carry

    def other_rows(b, carry):
        real, imag = gridded(b, 1)
        scale = jnp.where(b < live[0, 0], 2.0**-18, 0.0)
        out[0, 0, b, 0:1, :] = jnp.sum(acc[b, 0] + real, axis=0, keepdims=True) * scale
        out[0, 0, b, 1:2, :] = jnp.sum(acc[b, 1] + imag, axis=0, keepdims=True) * scale
        return carry

    turn_lines(core, 0)
    lax.fori_loop(0, NB, own_rows, 0, unroll=16)
    phase3(1 - core).wait_recv()
    turn_lines(1 - core, 1)
    lax.fori_loop(0, NB, other_rows, 0, unroll=16)

    for copy in sent1:
        copy.wait_send()
    for there in others_xy:
        phase2(here, there // NY, lax.rem(there, NY)).wait_send()
    sent3.wait_send()


def per_device(sky, col, rows, cnt, ws, live, codes, crd):
    hbm = pl.BlockSpec(memory_space=pl.ANY)
    dma = pltpu.SemaphoreType.DMA
    return pl.pallas_call(
        kernel,
        out_shape=jax.ShapeDtypeStruct((1, 1, NB, 2, NV), F32),
        in_specs=[hbm] * 9,
        out_specs=pl.BlockSpec(memory_space=pltpu.VMEM),
        scratch_shapes=[
            pltpu.VMEM((4, 2048), F32),
            pltpu.VMEM((64, 128), F32),
            pltpu.VMEM((256, 2 * SG), BF16),
            pltpu.VMEM((1, 1, NB, 2, NV), F32),
            pltpu.SMEM((32,), jnp.int32),
            pltpu.SMEM((8,), jnp.int32),
            pltpu.SMEM((1, 1), jnp.int32),
            pltpu.SMEM((1, 1, 8), jnp.int32),
            pltpu.SMEM((1, 1), jnp.int32),
            pltpu.SMEM((1, 1, NB), jnp.int32),
            pltpu.VMEM((NZ, 32, 256), BF16),
            pltpu.VMEM((256, 2 * SG), F32),
            pltpu.VMEM((NX, 2, 8, SG), F32),
            pltpu.VMEM((NX, 2, 8, SG), F32),
            pltpu.VMEM((NX, 64, SG), BF16),
            pltpu.VMEM((NX, 16, HALF), BF16),
            pltpu.VMEM((NX * NY, 16, HALF), BF16),
            pltpu.VMEM((2, NY, 16, HALF), BF16),
            pltpu.VMEM((8, 2, 8, HALF), F32),
            pltpu.VMEM((8, 2, 128, 256), BF16),
            pltpu.VMEM((NB, 2 * NV, 2 * NV), BF16),
            pltpu.VMEM((NB, 128, NV), F32),
            pltpu.VMEM((NB, 2, 8, NV), F32),
            pltpu.SMEM((NB,), jnp.int32),
            pltpu.VMEM((NB, 2, 8, NV), F32),
            dma((9,)), dma((NZ,)), dma((NZ,)), dma((NX * NY,)), dma((NX * NY,)), dma, dma,
        ],
        compiler_params=pltpu.CompilerParams(collective_id=0, has_side_effects=True, vmem_limit_bytes=60 * 2**20),
    )(sky, col, rows, cnt, ws, live, codes, crd, jnp.asarray(dft_table()))


def solution(mesh):
    placed = (
        P("fy", "fx"), P(), P(), P("fx", "fy"), P("fx", "fy", None), P("fx", "fy"), P("fx", "fy", None),
        P("fx", "fy", None, None, None),
    )
    return jax.shard_map(
        per_device, mesh=mesh, in_specs=placed, out_specs=P("fx", "fy", None, None, None), check_vma=False
    )
```

```python
import functools

import jax
import jax.numpy as jnp
import numpy as np
from jax import lax
from jax.experimental import pallas as pl
from jax.experimental.pallas import tpu as pltpu
from jax.sharding import PartitionSpec as P

MESH = pl.DeviceIdType.MESH
SG = 1024
NSKY = 65536
NB = 16
NV = 128
SG0 = 32
NX = 4
NZ = 8
NY = 4
NQ = 8
HALF = SG // 2
F32 = jnp.float32
BF16 = jnp.bfloat16
SIN = (3.141592502593994, -5.167698860168457, 2.5499982833862305, -0.59855055809021, 0.0807478204369545, -0.00608947454020381)
COS = (1.0, -4.93480110168457, 4.058694839477539, -1.3351584672927856, 0.23502980172634125, -0.025358984246850014, 0.0015939107397571206)


def cis(turns):
    near = turns - jnp.floor(turns + 0.5)
    y = near + near
    z = y * y
    sine = jnp.full_like(z, SIN[-1])
    for c in SIN[-2::-1]:
        sine = sine * z + c
    cosine = jnp.full_like(z, COS[-1])
    for c in COS[-2::-1]:
        cosine = cosine * z + c
    return cosine, sine * y


def dft_table():
    row = np.arange(NZ * 32)
    b = 128 * (row // 32) + 2 * (row % 16) + (row // 16) % 2
    angle = (b[:, None] * np.arange(SG)[None, :]) % SG * (2 * np.pi / SG)
    return np.concatenate([np.cos(angle), -np.sin(angle)], axis=1).astype(BF16)


def iota(shape, axis):
    return lax.broadcasted_iota(jnp.int32, shape, axis)


def kernel(
    sky_h, col_h, row_h, cnt_h, ws_h, live_h, codes_h, crd_h, tab_h, out,
    sky, tmp, tab, crd, col, rows, cnt, ws, live, codes, gath, spec, w8, tw, ybuf, part, got, strips, cross, lines, fine, vtab, wtab, form, acc,
    load_sem, send1, recv1, send2, recv2, send3, recv3,
):
    fx, fy = lax.axis_index("fx"), lax.axis_index("fy")
    z, x = fx // NX, lax.rem(fx, NX)
    y, core = fy // 2, lax.rem(fy, 2)

    along_z = [(lax.rem(z + d, NZ) * NX + x, fy) for d in range(1, NZ)]
    plane = {
        (dx, dy): (z * NX + lax.rem(x + dx, NX), lax.rem(y + dy, NY) * 2 + core)
        for dx in (2, 1, 3, 0) for dy in (2, 1, 3, 0) if dx or dy
    }
    other = (fx, y * 2 + 1 - core)
    peers = [along_z[d - 1] for d in (4, 3, 5, 2, 6, 1, 7)] + list(plane.values()) + [other]
    barrier = pltpu.get_barrier_semaphore()
    for peer in peers:
        pl.semaphore_signal(barrier, inc=1, device_id=peer, device_id_type=MESH)

    pairs = [(sky_h, sky), (col_h, col), (row_h, rows), (cnt_h, cnt), (ws_h, ws), (live_h, live), (codes_h, codes), (crd_h, crd), (tab_h, tab)]
    loads = [pltpu.make_async_copy(a, b, load_sem.at[i]) for i, (a, b) in enumerate(pairs)]
    for load in loads:
        load.start()

    loads[0].wait()
    for j in range(16):
        tmp[4 * j : 4 * j + 4, :] = sky[:, 128 * j : 128 * j + 128]
    left = iota((16, 128), 1) < 64
    line = [tmp[pl.ds(i, 16, stride=4), :] for i in range(4)]
    turned = [pltpu.roll(a, 64, 1) for a in line]
    halves = []
    for i in (0, 2):
        low = jnp.where(left, line[i], turned[i + 1])
        high = jnp.where(left, turned[i], line[i + 1])
        halves.append(jnp.concatenate([low, high], axis=0))
    gath[z] = jnp.concatenate(halves, axis=1).astype(BF16)

    for load in loads[1:]:
        load.wait()

    kappa = iota((8, SG), 1)
    c0 = iota((8, SG), 0)

    def wave(off):
        return off + jnp.bitwise_and(kappa - off, SG - 1)

    for d in range(NX):
        k = wave(col[z * NX + d])
        cosine, sine = cis(jnp.bitwise_and(k * 8, NSKY - 1).astype(F32) * (1.0 / NSKY))
        w8[d, 0] = cosine
        w8[d, 1] = -sine
        cosine, sine = cis(jnp.bitwise_and(c0 * k + 2048 * x * kappa, NSKY - 1).astype(F32) * (1.0 / NSKY))
        tw[d, 0] = cosine
        tw[d, 1] = -sine

    pl.semaphore_wait(barrier, len(peers))

    def phase1(slot, there):
        return pltpu.make_async_remote_copy(
            src_ref=gath.at[slot], dst_ref=gath.at[slot], send_sem=send1.at[there], recv_sem=recv1.at[slot],
            device_id=(there * NX + x, fy), device_id_type=MESH,
        )

    others_z = [j + (z <= j).astype(jnp.int32) for j in range(NZ - 1)]
    sent1 = [phase1(z, there) for there in others_z]
    for copy in sent1:
        copy.start()
    side = iota((8, HALF), 1)
    high = 2 * (side // 128) + iota((8, HALF), 0) // 4 - 4
    for r in range(8):
        mixed = jnp.bitwise_and(r * high * jnp.bitwise_and(side, 127), 7)
        cosine, sine = cis(mixed.astype(F32) * 0.125)
        cross[r, 0] = cosine
        cross[r, 1] = sine

    r = iota((128, 64), 0)
    m = iota((128, 64), 1)
    q = 2 * (jnp.bitwise_and(r, 31) // 8) + jnp.where(jnp.bitwise_and(r, 32) == 0, core, 1 - core)
    i = jnp.bitwise_and(r, 3)
    turn = jnp.bitwise_and((q * (NSKY // NQ) + i) * (rows[fy] + jnp.bitwise_and(m, 31)), NSKY - 1)
    quarter = (m >= 32).astype(jnp.int32) - (r >= 64).astype(jnp.int32)
    wide = cis(quarter.astype(F32) * 0.25 - turn.astype(F32) * (1.0 / NSKY))[0].astype(BF16)

    count = cnt[0, 0]
    g = iota((NV, NV), 0)
    m = iota((SG0, NV), 0)
    odd = (jnp.bitwise_and(iota((64, NV), 0), 4) * 32).astype(F32)

    def depth_of(b):
        plane = lax.rem(codes[0, 0, b], count)
        depth = jnp.int32(0)
        for layer in range(8):
            depth = depth + jnp.where(layer <= plane, ws[0, 0, layer], 0)
        return depth

    def fill(b, carry):
        depth = depth_of(b)
        u = crd[0, 0, b, 0:1, :]
        v = crd[0, 0, b, 1:2, :]
        screen = jnp.bitwise_and(depth * (m - 16) * (m - 16), 2047).astype(F32) * (1.0 / 2048)
        wave_real, wave_imag = cis(m.astype(F32) * u + screen)
        both = jnp.concatenate([wave_real, wave_imag], axis=0).astype(BF16)
        turned = jnp.dot(wide, both, preferred_element_type=F32)
        cosine, sine = cis(256.0 * jnp.broadcast_to(v, (8, NV)))
        wtab[b, 0] = cosine
        wtab[b, 1] = sine
        form[b] = jnp.bitwise_and(depth, 7)
        cosine, sine = cis(odd * v)
        vtab[b, 0:64] = turned[:64] * cosine - turned[64:] * sine
        vtab[b, 64:128] = turned[:64] * sine + turned[64:] * cosine
        screen = jnp.bitwise_and(depth * g * g, 2047).astype(F32) * (1.0 / 2048)
        cosine, sine = cis(g.astype(F32) * v + screen)
        fine[b, 0:NV, 0:NV] = cosine.astype(BF16)
        fine[b, 0:NV, NV : 2 * NV] = sine.astype(BF16)
        fine[b, NV : 2 * NV, 0:NV] = (-sine).astype(BF16)
        fine[b, NV : 2 * NV, NV : 2 * NV] = cosine.astype(BF16)
        return carry

    lax.fori_loop(0, 8, fill, 0)

    for there in others_z:
        phase1(there, there).wait_recv()

    sky_t = gath[...].reshape(NZ * 32, 256)
    for lo in (0, HALF):
        for plus in (0, SG):
            cols = slice(lo + plus, lo + plus + HALF)
            spec[:, cols] = lax.dot_general(sky_t, tab[:, cols], (((0,), (0,)), ((), ())), preferred_element_type=F32)
    pick_row = iota((8, 64), 0)
    pick_col = iota((8, 64), 1)
    pick = jnp.where(
        (pick_col // 16 == jnp.bitwise_and(pick_row, 3)) & (jnp.bitwise_and(pick_col // 8, 1) == pick_row // 4), 1.0, 0.0
    ).astype(BF16)

    def phase2(slot, to_x, to_y):
        return pltpu.make_async_remote_copy(
            src_ref=part.at[to_x], dst_ref=got.at[slot], send_sem=send2.at[NY * to_x + to_y], recv_sem=recv2.at[slot],
            device_id=(z * NX + to_x, to_y * 2 + core), device_id_type=MESH,
        )

    here = NY * x + y
    others_xy = [j + (here <= j).astype(jnp.int32) for j in range(NX * NY - 1)]
    for d in range(NX):
        def facet_row(step, carry):
            x0, lo = step % 4, HALF * (step // 4)
            for lo in (lo,):
                cols = slice(lo, lo + HALF)
                wr, wi = w8[d, 0, :, cols], w8[d, 1, :, cols]

                def at(c1, plus):
                    return spec[x0 * 64 + 8 * c1 : x0 * 64 + 8 * c1 + 8, lo + plus : lo + plus + HALF]

                ar, ai = at(7, 0), at(7, SG)
                for c1 in range(6, -1, -1):
                    ar, ai = ar * wr - ai * wi + at(c1, 0), ar * wi + ai * wr + at(c1, SG)
                tr, ti = tw[d, 0, :, cols], tw[d, 1, :, cols]
                both = jnp.concatenate([ar * tr - ai * ti, ar * ti + ai * tr], axis=0)
                ybuf[d, 16 * x0 : 16 * x0 + 16, cols] = both.astype(BF16)
            return carry

        for step in range(8):
            facet_row(step, 0)
        strip = jnp.dot(pick, ybuf[d], preferred_element_type=F32)
        packed = jnp.concatenate([strip[:, :HALF], strip[:, HALF:]], axis=0)
        part[d] = packed.astype(BF16)
        for to_y in range(NY):
            @pl.when(jnp.logical_or(x != d, y != to_y))
            def send():
                phase2(here, d, to_y).start()

    got[here] = part[x]
    lax.fori_loop(8, NB, fill, 0)
    for there in others_xy:
        phase2(there, there // NY, lax.rem(there, NY)).wait_recv()

    totals = []
    for dy in range(NY):
        total = got[dy].astype(F32)
        for dx in range(1, NX):
            total = total + got[NY * dx + dy].astype(F32)
        totals.append(jnp.concatenate([total[:8], total[8:]], axis=1))
    shift = jnp.bitwise_and(SG - jnp.bitwise_and(col[fx], SG - 1), SG - 1)
    ordered = pltpu.roll(jnp.concatenate(totals, axis=0), shift, 1)
    upper = iota((8, 128), 0) < 4
    for dy in range(NY):
        flat = ordered[8 * dy : 8 * dy + 8]
        real, imag = [], []
        for hh in range(4):
            even, odd_h = flat[:, 256 * hh : 256 * hh + 128], flat[:, 256 * hh + 128 : 256 * hh + 256]
            real.append(jnp.where(upper, even, pltpu.roll(odd_h, 4, 0)))
            imag.append(jnp.where(upper, pltpu.roll(even, 4, 0), odd_h))
        packed = jnp.concatenate([jnp.concatenate(real, axis=1), jnp.concatenate(imag, axis=1)], axis=0)
        strips[core, dy] = packed.astype(BF16)

    def phase3(slot):
        return pltpu.make_async_remote_copy(
            src_ref=strips.at[slot], dst_ref=strips.at[slot], send_sem=send3, recv_sem=recv3,
            device_id=other, device_id_type=MESH,
        )

    sent3 = phase3(core)
    sent3.start()

    def turn_lines(where, half):
        for hh in range(4):
            cols = slice(128 * hh, 128 * hh + 128)
            rows_at = slice(32 * hh, 32 * hh + 32)
            block = strips[where, :, :, cols].astype(F32)
            real, imag = block[:, 0:8, :], block[:, 8:16, :]
            for r in range(8):
                cosine, sine = cross[r, 0:1, :, cols], cross[r, 1:2, :, cols]
                lines[r, half, rows_at, 0:128] = (real * cosine - imag * sine).reshape(32, 128).astype(BF16)
                lines[r, half, rows_at, 128:256] = (real * sine + imag * cosine).reshape(32, 128).astype(BF16)

    def gridded(b, half):
        prod = jnp.dot(lines[form[b], half], fine[b], preferred_element_type=F32)
        wr, wi = wtab[b, 0:1], wtab[b, 1:2]

        def tile(hh, lo):
            return prod[32 * hh : 32 * hh + 32, lo : lo + NV].reshape(4, 8, NV)

        ar, ai = tile(3, 0), tile(3, NV)
        for hh in (2, 1, 0):
            ar, ai = ar * wr - ai * wi + tile(hh, 0), ar * wi + ai * wr + tile(hh, NV)
        at = 32 * half
        vr, vi = vtab[b, at : at + 32].reshape(4, 8, NV), vtab[b, 64 + at : 96 + at].reshape(4, 8, NV)
        return jnp.sum(vr * ar - vi * ai, axis=0), jnp.sum(vr * ai + vi * ar, axis=0)

    def own_rows(b, carry):
        acc[b, 0], acc[b, 1] = gridded(b, 0)
        return carry

    def other_rows(b, carry):
        real, imag = gridded(b, 1)
        scale = jnp.where(b < live[0, 0], 2.0**-18, 0.0)
        out[0, 0, b, 0:1, :] = jnp.sum(acc[b, 0] + real, axis=0, keepdims=True) * scale
        out[0, 0, b, 1:2, :] = jnp.sum(acc[b, 1] + imag, axis=0, keepdims=True) * scale
        return carry

    turn_lines(core, 0)
    lax.fori_loop(0, NB, own_rows, 0, unroll=16)
    phase3(1 - core).wait_recv()
    turn_lines(1 - core, 1)
    lax.fori_loop(0, NB, other_rows, 0, unroll=16)

    for copy in sent1:
        copy.wait_send()
    for there in others_xy:
        phase2(here, there // NY, lax.rem(there, NY)).wait_send()
    sent3.wait_send()


def per_device(sky, col, rows, cnt, ws, live, codes, crd):
    hbm = pl.BlockSpec(memory_space=pl.ANY)
    dma = pltpu.SemaphoreType.DMA
    return pl.pallas_call(
        kernel,
        out_shape=jax.ShapeDtypeStruct((1, 1, NB, 2, NV), F32),
        in_specs=[hbm] * 9,
        out_specs=pl.BlockSpec(memory_space=pltpu.VMEM),
        scratch_shapes=[
            pltpu.VMEM((4, 2048), F32),
            pltpu.VMEM((64, 128), F32),
            pltpu.VMEM((256, 2 * SG), BF16),
            pltpu.VMEM((1, 1, NB, 2, NV), F32),
            pltpu.SMEM((32,), jnp.int32),
            pltpu.SMEM((8,), jnp.int32),
            pltpu.SMEM((1, 1), jnp.int32),
            pltpu.SMEM((1, 1, 8), jnp.int32),
            pltpu.SMEM((1, 1), jnp.int32),
            pltpu.SMEM((1, 1, NB), jnp.int32),
            pltpu.VMEM((NZ, 32, 256), BF16),
            pltpu.VMEM((256, 2 * SG), F32),
            pltpu.VMEM((NX, 2, 8, SG), F32),
            pltpu.VMEM((NX, 2, 8, SG), F32),
            pltpu.VMEM((NX, 64, SG), BF16),
            pltpu.VMEM((NX, 16, HALF), BF16),
            pltpu.VMEM((NX * NY, 16, HALF), BF16),
            pltpu.VMEM((2, NY, 16, HALF), BF16),
            pltpu.VMEM((8, 2, 8, HALF), F32),
            pltpu.VMEM((8, 2, 128, 256), BF16),
            pltpu.VMEM((NB, 2 * NV, 2 * NV), BF16),
            pltpu.VMEM((NB, 128, NV), F32),
            pltpu.VMEM((NB, 2, 8, NV), F32),
            pltpu.SMEM((NB,), jnp.int32),
            pltpu.VMEM((NB, 2, 8, NV), F32),
            dma((9,)), dma((NZ,)), dma((NZ,)), dma((NX * NY,)), dma((NX * NY,)), dma, dma,
        ],
        compiler_params=pltpu.CompilerParams(collective_id=0, has_side_effects=True, vmem_limit_bytes=60 * 2**20),
    )(sky, col, rows, cnt, ws, live, codes, crd, jnp.asarray(dft_table()))


def solution(mesh):
    placed = (
        P("fy", "fx"), P(), P(), P("fx", "fy"), P("fx", "fy", None), P("fx", "fy"), P("fx", "fy", None),
        P("fx", "fy", None, None, None),
    )
    return jax.shard_map(
        per_device, mesh=mesh, in_specs=placed, out_specs=P("fx", "fy", None, None, None), check_vma=False
    )
```

```python
import functools

import jax
import jax.numpy as jnp
import numpy as np
from jax import lax
from jax.experimental import pallas as pl
from jax.experimental.pallas import tpu as pltpu
from jax.sharding import PartitionSpec as P

MESH = pl.DeviceIdType.MESH
SG = 1024
NSKY = 65536
NB = 16
NV = 128
SG0 = 32
NX = 4
NZ = 8
NY = 4
NQ = 8
HALF = SG // 2
F32 = jnp.float32
BF16 = jnp.bfloat16
SIN = (3.141592502593994, -5.167698860168457, 2.5499982833862305, -0.59855055809021, 0.0807478204369545, -0.00608947454020381)
COS = (1.0, -4.93480110168457, 4.058694839477539, -1.3351584672927856, 0.23502980172634125, -0.025358984246850014, 0.0015939107397571206)


def cis(turns):
    near = turns - jnp.floor(turns + 0.5)
    y = near + near
    z = y * y
    sine = jnp.full_like(z, SIN[-1])
    for c in SIN[-2::-1]:
        sine = sine * z + c
    cosine = jnp.full_like(z, COS[-1])
    for c in COS[-2::-1]:
        cosine = cosine * z + c
    return cosine, sine * y


def dft_table():
    row = np.arange(NZ * 32)
    b = 128 * (row // 32) + 2 * (row % 16) + (row // 16) % 2
    angle = (b[:, None] * np.arange(SG)[None, :]) % SG * (2 * np.pi / SG)
    return np.concatenate([np.cos(angle), -np.sin(angle)], axis=1).astype(BF16)


def iota(shape, axis):
    return lax.broadcasted_iota(jnp.int32, shape, axis)


def kernel(
    sky_h, col_h, row_h, cnt_h, ws_h, live_h, codes_h, crd_h, tab_h, out,
    sky, tmp, tab, crd, col, rows, cnt, ws, live, codes, gath, spec, w8, tw, ybuf, part, got, strips, cross, lines, fine, vtab, wtab, form, acc,
    load_sem, send1, recv1, send2, recv2, send3, recv3,
):
    fx, fy = lax.axis_index("fx"), lax.axis_index("fy")
    z, x = fx // NX, lax.rem(fx, NX)
    y, core = fy // 2, lax.rem(fy, 2)

    along_z = [(lax.rem(z + d, NZ) * NX + x, fy) for d in range(1, NZ)]
    plane = {
        (dx, dy): (z * NX + lax.rem(x + dx, NX), lax.rem(y + dy, NY) * 2 + core)
        for dx in (2, 1, 3, 0) for dy in (2, 1, 3, 0) if dx or dy
    }
    other = (fx, y * 2 + 1 - core)
    peers = [along_z[d - 1] for d in (4, 3, 5, 2, 6, 1, 7)] + list(plane.values()) + [other]
    barrier = pltpu.get_barrier_semaphore()
    for peer in peers:
        pl.semaphore_signal(barrier, inc=1, device_id=peer, device_id_type=MESH)

    pairs = [(sky_h, sky), (col_h, col), (row_h, rows), (cnt_h, cnt), (ws_h, ws), (live_h, live), (codes_h, codes), (crd_h, crd), (tab_h, tab)]
    loads = [pltpu.make_async_copy(a, b, load_sem.at[i]) for i, (a, b) in enumerate(pairs)]
    for load in loads:
        load.start()

    loads[0].wait()
    for j in range(16):
        tmp[4 * j : 4 * j + 4, :] = sky[:, 128 * j : 128 * j + 128]
    left = iota((16, 128), 1) < 64
    line = [tmp[pl.ds(i, 16, stride=4), :] for i in range(4)]
    turned = [pltpu.roll(a, 64, 1) for a in line]
    halves = []
    for i in (0, 2):
        low = jnp.where(left, line[i], turned[i + 1])
        high = jnp.where(left, turned[i], line[i + 1])
        halves.append(jnp.concatenate([low, high], axis=0))
    gath[z] = jnp.concatenate(halves, axis=1).astype(BF16)

    for load in loads[1:]:
        load.wait()

    kappa = iota((8, SG), 1)
    c0 = iota((8, SG), 0)

    def wave(off):
        return off + jnp.bitwise_and(kappa - off, SG - 1)

    for d in range(NX):
        k = wave(col[z * NX + d])
        cosine, sine = cis(jnp.bitwise_and(k * 8, NSKY - 1).astype(F32) * (1.0 / NSKY))
        w8[d, 0] = cosine
        w8[d, 1] = -sine
        cosine, sine = cis(jnp.bitwise_and(c0 * k + 2048 * x * kappa, NSKY - 1).astype(F32) * (1.0 / NSKY))
        tw[d, 0] = cosine
        tw[d, 1] = -sine

    pl.semaphore_wait(barrier, len(peers))

    def phase1(slot, there):
        return pltpu.make_async_remote_copy(
            src_ref=gath.at[slot], dst_ref=gath.at[slot], send_sem=send1.at[there], recv_sem=recv1.at[slot],
            device_id=(there * NX + x, fy), device_id_type=MESH,
        )

    others_z = [j + (z <= j).astype(jnp.int32) for j in range(NZ - 1)]
    sent1 = [phase1(z, there) for there in others_z]
    for copy in sent1:
        copy.start()
    side = iota((8, HALF), 1)
    high = 2 * (side // 128) + iota((8, HALF), 0) // 4 - 4
    for r in range(8):
        mixed = jnp.bitwise_and(r * high * jnp.bitwise_and(side, 127), 7)
        cosine, sine = cis(mixed.astype(F32) * 0.125)
        cross[r, 0] = cosine
        cross[r, 1] = sine

    r = iota((128, 64), 0)
    m = iota((128, 64), 1)
    q = 2 * (jnp.bitwise_and(r, 31) // 8) + jnp.where(jnp.bitwise_and(r, 32) == 0, core, 1 - core)
    i = jnp.bitwise_and(r, 3)
    turn = jnp.bitwise_and((q * (NSKY // NQ) + i) * (rows[fy] + jnp.bitwise_and(m, 31)), NSKY - 1)
    quarter = (m >= 32).astype(jnp.int32) - (r >= 64).astype(jnp.int32)
    wide = cis(quarter.astype(F32) * 0.25 - turn.astype(F32) * (1.0 / NSKY))[0].astype(BF16)

    count = cnt[0, 0]
    g = iota((NV, NV), 0)
    m = iota((SG0, NV), 0)
    odd = (jnp.bitwise_and(iota((8, NV), 0), 4) * 32).astype(F32)

    def depth_of(b):
        plane = lax.rem(codes[0, 0, b], count)
        depth = jnp.int32(0)
        for layer in range(8):
            depth = depth + jnp.where(layer <= plane, ws[0, 0, layer], 0)
        return depth

    def fill(b, carry):
        depth = depth_of(b)
        u = crd[0, 0, b, 0:1, :]
        v = crd[0, 0, b, 1:2, :]
        screen = jnp.bitwise_and(depth * (m - 16) * (m - 16), 2047).astype(F32) * (1.0 / 2048)
        wave_real, wave_imag = cis(m.astype(F32) * u + screen)
        both = jnp.concatenate([wave_real, wave_imag], axis=0).astype(BF16)
        turned = jnp.dot(wide, both, preferred_element_type=F32)
        cosine, sine = cis(256.0 * jnp.broadcast_to(v, (8, NV)))
        wtab[b, 0] = cosine
        wtab[b, 1] = sine
        form[b] = jnp.bitwise_and(depth, 7)
        cosine, sine = cis(odd * v)
        real, imag = turned[:64].reshape(8, 8, NV), turned[64:].reshape(8, 8, NV)
        vtab[b, 0:64] = (real * cosine[None] - imag * sine[None]).reshape(64, NV)
        vtab[b, 64:128] = (real * sine[None] + imag * cosine[None]).reshape(64, NV)
        screen = jnp.bitwise_and(depth * g * g, 2047).astype(F32) * (1.0 / 2048)
        cosine, sine = cis(g.astype(F32) * v + screen)
        fine[b, 0:NV, 0:NV] = cosine.astype(BF16)
        fine[b, 0:NV, NV : 2 * NV] = sine.astype(BF16)
        fine[b, NV : 2 * NV, 0:NV] = (-sine).astype(BF16)
        fine[b, NV : 2 * NV, NV : 2 * NV] = cosine.astype(BF16)
        return carry

    lax.fori_loop(0, 8, fill, 0)

    for there in others_z:
        phase1(there, there).wait_recv()

    sky_t = gath[...].reshape(NZ * 32, 256)
    for lo in (0, HALF):
        for plus in (0, SG):
            cols = slice(lo + plus, lo + plus + HALF)
            spec[:, cols] = lax.dot_general(sky_t, tab[:, cols], (((0,), (0,)), ((), ())), preferred_element_type=F32)
    pick_row = iota((8, 64), 0)
    pick_col = iota((8, 64), 1)
    pick = jnp.where(
        (pick_col // 16 == jnp.bitwise_and(pick_row, 3)) & (jnp.bitwise_and(pick_col // 8, 1) == pick_row // 4), 1.0, 0.0
    ).astype(BF16)

    def phase2(slot, to_x, to_y):
        return pltpu.make_async_remote_copy(
            src_ref=part.at[to_x], dst_ref=got.at[slot], send_sem=send2.at[NY * to_x + to_y], recv_sem=recv2.at[slot],
            device_id=(z * NX + to_x, to_y * 2 + core), device_id_type=MESH,
        )

    here = NY * x + y
    others_xy = [j + (here <= j).astype(jnp.int32) for j in range(NX * NY - 1)]
    for d in range(NX):
        def facet_row(step, carry):
            x0, lo = step % 4, HALF * (step // 4)
            for lo in (lo,):
                cols = slice(lo, lo + HALF)
                wr, wi = w8[d, 0, :, cols], w8[d, 1, :, cols]

                def at(c1, plus):
                    return spec[x0 * 64 + 8 * c1 : x0 * 64 + 8 * c1 + 8, lo + plus : lo + plus + HALF]

                ar, ai = at(7, 0), at(7, SG)
                for c1 in range(6, -1, -1):
                    ar, ai = ar * wr - ai * wi + at(c1, 0), ar * wi + ai * wr + at(c1, SG)
                tr, ti = tw[d, 0, :, cols], tw[d, 1, :, cols]
                both = jnp.concatenate([ar * tr - ai * ti, ar * ti + ai * tr], axis=0)
                ybuf[d, 16 * x0 : 16 * x0 + 16, cols] = both.astype(BF16)
            return carry

        for step in range(8):
            facet_row(step, 0)
        strip = jnp.dot(pick, ybuf[d], preferred_element_type=F32)
        packed = jnp.concatenate([strip[:, :HALF], strip[:, HALF:]], axis=0)
        part[d] = packed.astype(BF16)
        for to_y in range(NY):
            @pl.when(jnp.logical_or(x != d, y != to_y))
            def send():
                phase2(here, d, to_y).start()

    got[here] = part[x]
    lax.fori_loop(8, NB, fill, 0)
    for there in others_xy:
        phase2(there, there // NY, lax.rem(there, NY)).wait_recv()

    totals = []
    for dy in range(NY):
        total = got[dy].astype(F32)
        for dx in range(1, NX):
            total = total + got[NY * dx + dy].astype(F32)
        totals.append(jnp.concatenate([total[:8], total[8:]], axis=1))
    shift = jnp.bitwise_and(SG - jnp.bitwise_and(col[fx], SG - 1), SG - 1)
    ordered = pltpu.roll(jnp.concatenate(totals, axis=0), shift, 1)
    upper = iota((8, 128), 0) < 4
    for dy in range(NY):
        flat = ordered[8 * dy : 8 * dy + 8]
        real, imag = [], []
        for hh in range(4):
            even, odd_h = flat[:, 256 * hh : 256 * hh + 128], flat[:, 256 * hh + 128 : 256 * hh + 256]
            real.append(jnp.where(upper, even, pltpu.roll(odd_h, 4, 0)))
            imag.append(jnp.where(upper, pltpu.roll(even, 4, 0), odd_h))
        packed = jnp.concatenate([jnp.concatenate(real, axis=1), jnp.concatenate(imag, axis=1)], axis=0)
        strips[core, dy] = packed.astype(BF16)

    def phase3(slot):
        return pltpu.make_async_remote_copy(
            src_ref=strips.at[slot], dst_ref=strips.at[slot], send_sem=send3, recv_sem=recv3,
            device_id=other, device_id_type=MESH,
        )

    sent3 = phase3(core)
    sent3.start()

    def turn_lines(where, half):
        for hh in range(4):
            cols = slice(128 * hh, 128 * hh + 128)
            rows_at = slice(32 * hh, 32 * hh + 32)
            block = strips[where, :, :, cols].astype(F32)
            real, imag = block[:, 0:8, :], block[:, 8:16, :]
            for r in range(8):
                cosine, sine = cross[r, 0:1, :, cols], cross[r, 1:2, :, cols]
                lines[r, half, rows_at, 0:128] = (real * cosine - imag * sine).reshape(32, 128).astype(BF16)
                lines[r, half, rows_at, 128:256] = (real * sine + imag * cosine).reshape(32, 128).astype(BF16)

    def gridded(b, half):
        prod = jnp.dot(lines[form[b], half], fine[b], preferred_element_type=F32)
        wr, wi = wtab[b, 0:1], wtab[b, 1:2]

        def tile(hh, lo):
            return prod[32 * hh : 32 * hh + 32, lo : lo + NV].reshape(4, 8, NV)

        ar, ai = tile(3, 0), tile(3, NV)
        for hh in (2, 1, 0):
            ar, ai = ar * wr - ai * wi + tile(hh, 0), ar * wi + ai * wr + tile(hh, NV)
        at = 32 * half
        vr, vi = vtab[b, at : at + 32].reshape(4, 8, NV), vtab[b, 64 + at : 96 + at].reshape(4, 8, NV)
        return jnp.sum(vr * ar - vi * ai, axis=0), jnp.sum(vr * ai + vi * ar, axis=0)

    def own_rows(b, carry):
        acc[b, 0], acc[b, 1] = gridded(b, 0)
        return carry

    def other_rows(b, carry):
        real, imag = gridded(b, 1)
        scale = jnp.where(b < live[0, 0], 2.0**-18, 0.0)
        out[0, 0, b, 0:1, :] = jnp.sum(acc[b, 0] + real, axis=0, keepdims=True) * scale
        out[0, 0, b, 1:2, :] = jnp.sum(acc[b, 1] + imag, axis=0, keepdims=True) * scale
        return carry

    turn_lines(core, 0)
    lax.fori_loop(0, NB, own_rows, 0, unroll=16)
    phase3(1 - core).wait_recv()
    turn_lines(1 - core, 1)
    lax.fori_loop(0, NB, other_rows, 0, unroll=16)

    for copy in sent1:
        copy.wait_send()
    for there in others_xy:
        phase2(here, there // NY, lax.rem(there, NY)).wait_send()
    sent3.wait_send()


def per_device(sky, col, rows, cnt, ws, live, codes, crd):
    hbm = pl.BlockSpec(memory_space=pl.ANY)
    dma = pltpu.SemaphoreType.DMA
    return pl.pallas_call(
        kernel,
        out_shape=jax.ShapeDtypeStruct((1, 1, NB, 2, NV), F32),
        in_specs=[hbm] * 9,
        out_specs=pl.BlockSpec(memory_space=pltpu.VMEM),
        scratch_shapes=[
            pltpu.VMEM((4, 2048), F32),
            pltpu.VMEM((64, 128), F32),
            pltpu.VMEM((256, 2 * SG), BF16),
            pltpu.VMEM((1, 1, NB, 2, NV), F32),
            pltpu.SMEM((32,), jnp.int32),
            pltpu.SMEM((8,), jnp.int32),
            pltpu.SMEM((1, 1), jnp.int32),
            pltpu.SMEM((1, 1, 8), jnp.int32),
            pltpu.SMEM((1, 1), jnp.int32),
            pltpu.SMEM((1, 1, NB), jnp.int32),
            pltpu.VMEM((NZ, 32, 256), BF16),
            pltpu.VMEM((256, 2 * SG), F32),
            pltpu.VMEM((NX, 2, 8, SG), F32),
            pltpu.VMEM((NX, 2, 8, SG), F32),
            pltpu.VMEM((NX, 64, SG), BF16),
            pltpu.VMEM((NX, 16, HALF), BF16),
            pltpu.VMEM((NX * NY, 16, HALF), BF16),
            pltpu.VMEM((2, NY, 16, HALF), BF16),
            pltpu.VMEM((8, 2, 8, HALF), F32),
            pltpu.VMEM((8, 2, 128, 256), BF16),
            pltpu.VMEM((NB, 2 * NV, 2 * NV), BF16),
            pltpu.VMEM((NB, 128, NV), F32),
            pltpu.VMEM((NB, 2, 8, NV), F32),
            pltpu.SMEM((NB,), jnp.int32),
            pltpu.VMEM((NB, 2, 8, NV), F32),
            dma((9,)), dma((NZ,)), dma((NZ,)), dma((NX * NY,)), dma((NX * NY,)), dma, dma,
        ],
        compiler_params=pltpu.CompilerParams(collective_id=0, has_side_effects=True, vmem_limit_bytes=60 * 2**20),
    )(sky, col, rows, cnt, ws, live, codes, crd, jnp.asarray(dft_table()))


def solution(mesh):
    placed = (
        P("fy", "fx"), P(), P(), P("fx", "fy"), P("fx", "fy", None), P("fx", "fy"), P("fx", "fy", None),
        P("fx", "fy", None, None, None),
    )
    return jax.shard_map(
        per_device, mesh=mesh, in_specs=placed, out_specs=P("fx", "fy", None, None, None), check_vma=False
    )
```
